256 devices in a mesh: outer: 32 (over z, y_lo, core), inner: 8 (over y_hi, x).
Axes of the slice: x: 4, y: 4 (y_hi: 2, y_lo: 2; y = y_hi * 2 + y_lo), z: 8, core: 2. Of those that a mesh axis runs over, the one named last changes fastest.
Arguments:
- queries: bfloat16 [32768, 4096], P(('outer', 'inner')), may hold values from -6 to 6
- keys: bfloat16 [32768, 512], P(('outer', 'inner')), may hold values from -6 to 6
- values: bfloat16 [32768, 512], P(('outer', 'inner')), may hold values from -6 to 6
- dout: bfloat16 [32768, 4096], P(('outer', 'inner')), may hold values from -48 to 48
- attn_out: bfloat16 [32768, 4096], P(('outer', 'inner')), may hold values from -6 to 6
Outputs:
- grad_queries: bfloat16 [32768, 4096], P(('outer', 'inner'))
- grad_keys: bfloat16 [32768, 512], P(('outer', 'inner'))
- grad_values: bfloat16 [32768, 512], P(('outer', 'inner'))
The draws below stay inside these ranges and needn't reach their ends.
All inputs are finite; a program needn't handle non-finite values.
Results may differ from the reference program's by a relative error of at most 0.0051.
Values may be sent and summed in bfloat16 or wider, within the bound.
A program may use at most 128 MiB of HBM per device.

```python
import jax
import jax.numpy as jnp
from jax import lax

NH = 32
KV = 4
HD = 128
GROUP = 4096
SEQ = 32768


def draw_queries(key, part):
    key = jax.random.fold_in(key, 11)
    entries = jax.random.truncated_normal(key, -6.0, 6.0, (SEQ, NH * HD), jnp.float32)
    return entries.astype(jnp.bfloat16)


def draw_keys(key, part):
    key = jax.random.fold_in(key, 23)
    entries = jax.random.truncated_normal(key, -6.0, 6.0, (SEQ, KV * HD), jnp.float32)
    return entries.astype(jnp.bfloat16)


def level_of(key, shape, shards, least, top_value):
    gain, own = 1.0, jax.random.fold_in(key, 6)
    for axis_at, parts in shards:
        steps = jnp.exp(jax.random.uniform(jax.random.fold_in(own, axis_at), (parts,), jnp.float32, least / len(shards), top_value / len(shards)))
        gain = gain * jnp.repeat(steps, shape[axis_at] // parts).reshape([-1 if axis == axis_at else 1 for axis in range(len(shape))])
    return gain


def scatter_about(own_key, dims, scale, most, split=(), kind=jnp.bfloat16):
    values = scale * jax.random.normal(own_key, dims, jnp.float32)
    if split:
        values = values * level_of(own_key, dims, split, -0.22, 0.18)
    return jnp.clip(values, -most, most).astype(kind)


def setup_inputs(seed: int = 0) -> dict:
    arg_keys = jax.random.split(jax.random.key(seed), 6)
    return {
        "queries": draw_queries(jax.random.fold_in(arg_keys[5], 71), 0),
        "keys": draw_keys(jax.random.fold_in(arg_keys[5], 71), 0),
        "values": scatter_about(arg_keys[2], (SEQ, KV * HD), 1.0, 6.0, ((0, 256),)),
        "dout": scatter_about(arg_keys[3], (SEQ, NH * HD), 8.0, 48.0, ((0, 256),)),
        "attn_out": scatter_about(arg_keys[4], (SEQ, NH * HD), 1.0, 6.0, ((0, 256),)),
    }


def group_half(query_rows, key_rows, value_rows, dout_rows, output_rows):
    length = query_rows.shape[0]
    kv_heads = key_rows.shape[1] // HD
    repeat = NH // KV
    scaling = HD ** -0.5
    qblock = min(512, length)
    grad_k = jnp.zeros(key_rows.shape, jnp.float32)
    grad_v = jnp.zeros(value_rows.shape, jnp.float32)
    grad_q_parts = []
    for first_row in range(0, length, qblock):
        key_end = first_row + qblock
        q_float = query_rows[first_row:key_end].astype(jnp.float32).reshape(qblock, kv_heads, repeat, HD)
        d_float = dout_rows[first_row:key_end].astype(jnp.float32).reshape(qblock, kv_heads, repeat, HD)
        o_float = output_rows[first_row:key_end].astype(jnp.float32).reshape(qblock, kv_heads, repeat, HD)
        k_float = key_rows[:key_end].astype(jnp.float32).reshape(key_end, kv_heads, HD)
        v_float = value_rows[:key_end].astype(jnp.float32).reshape(key_end, kv_heads, HD)
        scores = jnp.einsum('qgrd,kgd->grqk', q_float, k_float) * scaling
        q_places = first_row + jnp.arange(qblock, dtype=jnp.int32)
        k_places = jnp.arange(key_end, dtype=jnp.int32)
        allowed = k_places[None, :] <= q_places[:, None]
        scores = jnp.where(allowed, scores, -1e30)
        row_max = jnp.max(scores, axis=-1, keepdims=True)
        row_exp = jnp.exp(scores - row_max)
        weights = row_exp / jnp.sum(row_exp, axis=-1, keepdims=True)
        probs_low = lax.optimization_barrier(weights.astype(jnp.bfloat16)).astype(jnp.float32)
        delta_rows = jnp.transpose(jnp.sum(d_float * o_float, axis=-1), (1, 2, 0))[..., None]
        dprobs = jnp.einsum('qgrd,kgd->grqk', d_float, v_float)
        dscores = weights * (dprobs - delta_rows)
        dscores = lax.optimization_barrier(dscores.astype(jnp.bfloat16)).astype(jnp.float32)
        grad_q_parts.append((jnp.einsum('grqk,kgd->qgrd', dscores, k_float) * scaling).reshape(qblock, -1))
        grad_k = grad_k.at[:key_end].add((jnp.einsum('grqk,qgrd->kgd', dscores, q_float) * scaling).reshape(key_end, -1))
        grad_v = grad_v.at[:key_end].add(jnp.einsum('grqk,qgrd->kgd', probs_low, d_float).reshape(key_end, -1))
    return jnp.concatenate(grad_q_parts, axis=0), grad_k, grad_v


def half_grads(query_cols, key_cols, value_cols, dout_cols, output_cols):
    groups = SEQ // GROUP

    def split_rows(array):
        return array.reshape(groups, GROUP, array.shape[1])

    def one_group(pieces):
        return group_half(pieces[0], pieces[1], pieces[2], pieces[3], pieces[4])

    grad_q, grad_k, grad_v = lax.map(one_group, (split_rows(query_cols), split_rows(key_cols), split_rows(value_cols), split_rows(dout_cols), split_rows(output_cols)))
    return grad_q.reshape(SEQ, -1), grad_k.reshape(SEQ, -1), grad_v.reshape(SEQ, -1)


def reference(queries, keys, values, dout, attn_out):
    q_cols = NH * HD // 2
    k_cols = KV * HD // 2
    half_len = GROUP // 2

    def forward_roll(array):
        return jnp.roll(array, -half_len, axis=0)

    def back_roll(array):
        return jnp.roll(array, half_len, axis=0)

    plain_q, plain_k, plain_v = half_grads(queries[:, :q_cols], keys[:, :k_cols], values[:, :k_cols], dout[:, :q_cols], attn_out[:, :q_cols])
    shift_q, shift_k, shift_v = half_grads(forward_roll(queries[:, q_cols:]), forward_roll(keys[:, k_cols:]), forward_roll(values[:, k_cols:]), forward_roll(dout[:, q_cols:]), forward_roll(attn_out[:, q_cols:]))
    grad_queries = jnp.concatenate([plain_q, back_roll(shift_q)], axis=1).astype(jnp.bfloat16)
    grad_keys = jnp.concatenate([plain_k, back_roll(shift_k)], axis=1).astype(jnp.bfloat16)
    grad_values = jnp.concatenate([plain_v, back_roll(shift_v)], axis=1).astype(jnp.bfloat16)
    return grad_queries, grad_keys, grad_values
```

```python
import functools

import jax
import jax.numpy as jnp
from jax import lax
from jax.experimental import pallas as pl
from jax.experimental.pallas import tpu as pltpu
from jax.sharding import PartitionSpec as P

HD = 128
REP = 8
TOK = 128
QC = REP * TOK
CH = 4
CK = CH * TOK
CB = 256
SCALE = HD**-0.5
C2 = SCALE * 1.4426950408889634
NEG = -1e30
MESH = pl.DeviceIdType.MESH
F32 = jnp.float32
BF16 = jnp.bfloat16


def split3(x):
    hi = x.astype(BF16).astype(F32)
    rest = x - hi
    mid = rest.astype(BF16).astype(F32)
    low = rest - mid
    row = lax.broadcasted_iota(jnp.int32, (HD, x.shape[1]), 0)
    out = jnp.where(row == 0, hi, jnp.where(row == 1, mid, jnp.where(row == 2, low, 0.0)))
    return out.astype(BF16)


def kernel(
    nhp,
    q_in, k_in, v_in, do_in, o_in,
    dq_out, dk_out, dv_out,
    kvpack, kvwin, ret, rbuf, q_st, do_st, o_st, q_rows, do_rows, qt, dt, dqt, dq_st,
    m8, l8, acc_k, acc_v, sum_kv,
    x_loc, x_send, x_recv, g_send, g_recv, r_send, r_recv, d_loc, d_send, d_recv,
):
    outer = lax.axis_index("outer")
    n = lax.axis_index("inner")
    core = lax.rem(outer, 2)
    other = 1 - core
    hp = lax.div(outer, 2)
    y_lo = lax.rem(hp, 2)

    def dev(hp_, core_, n_):
        return (lax.rem(hp_ + nhp, nhp) * 2 + core_, n_)

    def half_cols(half, cc):
        return pl.ds(pl.multiple_of(half * (2 * QC) + cc * QC, QC), QC)

    def yy_of(half):
        return jnp.where(half == 0, y_lo, 1 - y_lo)

    barrier = pltpu.get_barrier_semaphore()

    def greet(d, _):
        near, cc, nn = lax.div(d, 16) - 1, lax.rem(lax.div(d, 8), 2), lax.rem(d, 8)

        @pl.when(jnp.logical_not((near == 0) & (cc == core) & (nn == n)))
        def _():
            pl.semaphore_signal(barrier, inc=1, device_id=dev(hp + near, cc, nn), device_id_type=MESH)

        return 0

    lax.fori_loop(0, 48, greet, 0)

    sources = ((q_in, q_st), (do_in, do_st), (o_in, o_st))

    def own_copy(a, half):
        src, dst = sources[a]
        return pltpu.make_async_copy(src.at[:, half_cols(half, core)], dst.at[half, core], x_loc.at[a, half])

    def sib_copy(a, half):
        src, dst = sources[a]
        return pltpu.make_async_remote_copy(
            src_ref=src.at[:, half_cols(half, other)], dst_ref=dst.at[half, core],
            send_sem=x_send.at[a, half], recv_sem=x_recv.at[a, half],
            device_id=dev(hp, other, n), device_id_type=MESH)

    for a in range(3):
        for half in range(2):
            own_copy(a, half).start()
    for half in range(2):
        for cc in range(2):
            g = 2 * half + cc
            kvpack[half, cc, 0] = k_in[:, g * HD : (g + 1) * HD]
            kvpack[half, cc, 1] = v_in[:, g * HD : (g + 1) * HD]

    pl.semaphore_wait(barrier, 47)

    for a in range(3):
        for half in range(2):
            sib_copy(a, half).start()

    def gather_copy(half, p, cc, slot, to_hp, nn):
        return pltpu.make_async_remote_copy(
            src_ref=kvpack.at[half, cc], dst_ref=kvwin.at[half, p],
            send_sem=g_send.at[half, cc, slot], recv_sem=g_recv.at[half, p],
            device_id=dev(to_hp, cc, nn), device_id_type=MESH)

    def each_gather(half, act):
        yy = yy_of(half)
        p = 16 * yy + 8 * core + n

        def near(t, _):
            nn = lax.rem(n + t, 8)
            for cc in range(2):
                needed = (8 * core + n <= nn + 8) & jnp.logical_not((t == 0) & (core == cc))

                @pl.when(needed)
                def _():
                    act(gather_copy(half, p, cc, t, hp, nn))

            return 0

        def far(t, _):
            nn = lax.rem(n + t, 8)
            for cc in range(2):
                act(gather_copy(half, p, cc, 8 + t, hp + 1, nn))
            return 0

        lax.fori_loop(0, 8, near, 0)

        @pl.when(yy == 0)
        def _():
            lax.fori_loop(0, 8, far, 0)

    for half in range(2):
        each_gather(half, lambda copy: copy.start())
    for half in range(2):
        p = 16 * yy_of(half) + 8 * core + n
        kvwin[half, p] = kvpack[half, core]

    for a in range(3):
        for half in range(2):
            own_copy(a, half).wait()
            sib_copy(a, half).wait_recv()

    def prepare(i, _):
        half, b = lax.div(i, 2), lax.rem(i, 2)
        for h in range(REP):
            cols = slice(h * HD, (h + 1) * HD)
            qv = q_st[half, b, :, cols]
            dv = do_st[half, b, :, cols]
            q_rows[half, b, cols, :] = qv
            do_rows[half, b, cols, :] = dv
            qt[half, b, :HD, cols] = qv.T
            dt[half, b, :HD, cols] = dv.T
            prod = dv.astype(F32) * o_st[half, b, :, cols].astype(F32)
            delta = jnp.sum(prod.T, axis=0, keepdims=True)
            dt[half, b, HD:, cols] = split3(-delta)
        m8[half, b] = jnp.full((8, QC), NEG, F32)
        l8[half, b] = jnp.zeros((8, QC), F32)
        dqt[half, b] = jnp.zeros((HD, QC), F32)
        return 0

    lax.fori_loop(0, 4, prepare, 0)

    lane = lax.broadcasted_iota(jnp.int32, (CK, HD), 1)
    ones3 = jnp.where(lane < 3, 1.0, 0.0).astype(BF16)

    def allowed_at(j, pos):
        key = lax.broadcasted_iota(jnp.int32, (CK, CB), 0)
        tok = lax.rem(lax.broadcasted_iota(jnp.int32, (CK, CB), 1), TOK)
        return key - tok <= pos * TOK - j * CK

    def one_half(step, _):
        half = lax.rem(step + FIRST(y_lo), 2)
        yy = yy_of(half)
        pos0 = 16 * yy + n
        last = pos0 + 8
        own = pos0 + 8 * core
        n0 = lax.div(pos0, CH) + 1
        n1 = lax.div(last, CH) + 1

        def by_mask(j, work):
            for b, count in ((1, n1), (0, n0)):
                @pl.when(j == count - 1)
                def _():
                    work(b, True)

                @pl.when(j < count - 1)
                def _():
                    work(b, False)

        def stats(t, _):
            j = n1 - 1 - t
            for u in range(CH):
                w = j * CH + u

                @pl.when((w <= last) & (w != own))
                def _():
                    gather_copy(half, w, 0, 0, hp, n).wait_recv()

                @pl.when(w > last)
                def _():
                    kvwin[half, w] = jnp.zeros((2, TOK, HD), BF16)

            def work(b, masked):
                keys = kvwin[half, pl.ds(j * CH, CH), 0].reshape(CK, HD)
                if masked:
                    allowed = allowed_at(j, pos0 + 8 * b)
                for piece in range(QC // CB):
                    cols = slice(piece * CB, (piece + 1) * CB)
                    s = jnp.dot(keys, qt[half, b, :HD, cols], preferred_element_type=F32)
                    if masked:
                        s = jnp.where(allowed, s, NEG)
                    s = s.reshape(CK // 8, 8, CB)
                    old = m8[half, b, :, cols]
                    new = jnp.maximum(old, jnp.max(s, axis=0))
                    e = jnp.exp2((s - new[None]) * C2)
                    l8[half, b, :, cols] = l8[half, b, :, cols] * jnp.exp2((old - new) * C2) + jnp.sum(e, axis=0)
                    m8[half, b, :, cols] = new

            by_mask(j, work)
            return 0

        lax.fori_loop(0, n1, stats, 0)
        for b in range(2):
            top = jnp.max(m8[half, b], axis=0, keepdims=True)
            total = jnp.sum(l8[half, b] * jnp.exp2((m8[half, b] - top) * C2), axis=0, keepdims=True)
            qt[half, b, HD:, :] = split3(-(top + jnp.log(total) * (1.0 / SCALE)))

        def grads(t, _):
            j = n1 - 1 - t

            def work(b, masked):
                keys = kvwin[half, pl.ds(j * CH, CH), 0].reshape(CK, HD)
                vals = kvwin[half, pl.ds(j * CH, CH), 1].reshape(CK, HD)
                keys_t = keys.T
                keys_1 = jnp.concatenate([keys, ones3], axis=1)
                vals_1 = jnp.concatenate([vals, ones3], axis=1)
                if masked:
                    allowed = allowed_at(j, pos0 + 8 * b)
                probs, dscores = [], []
                for piece in range(QC // CB):
                    cols = slice(piece * CB, (piece + 1) * CB)
                    s = jnp.dot(keys_1, qt[half, b, :, cols], preferred_element_type=F32)
                    prob = jnp.exp2(s * C2)
                    if masked:
                        prob = jnp.where(allowed, prob, 0.0)
                    dp = jnp.dot(vals_1, dt[half, b, :, cols], preferred_element_type=F32)
                    ds = (prob * dp).astype(BF16)
                    dqt[half, b, :, cols] += jnp.dot(keys_t, ds, preferred_element_type=F32)
                    probs.append(prob.astype(BF16))
                    dscores.append(ds)
                dv = jnp.dot(jnp.concatenate(probs, axis=1), do_rows[half, b], preferred_element_type=F32)
                dk = jnp.dot(jnp.concatenate(dscores, axis=1), q_rows[half, b], preferred_element_type=F32)
                if b == 1:
                    acc_k[...] = dk
                    acc_v[...] = dv
                else:
                    acc_k[...] += dk
                    acc_v[...] += dv

            by_mask(j, work)
            for u in range(CH):
                w = j * CH + u

                @pl.when(w <= last)
                def _():
                    rows = slice(u * TOK, (u + 1) * TOK)
                    ret[half, w, 0] = (acc_k[rows] * SCALE).astype(BF16)
                    ret[half, w, 1] = acc_v[rows].astype(BF16)

                    @pl.when(w != own)
                    def _():
                        return_copy(half, w, yy).start()

            return 0

        lax.fori_loop(0, n1, grads, 0)

        for b in range(2):
            for h in range(REP):
                cols = slice(h * HD, (h + 1) * HD)
                dq_st[half, b, :, cols] = (dqt[half, b, :, cols] * SCALE).T.astype(BF16)
        dq_own(half).start()
        dq_sib(half).start()
        return 0

    def return_copy(half, w, yy):
        return pltpu.make_async_remote_copy(
            src_ref=ret.at[half, w], dst_ref=rbuf.at[half, core, 8 * yy + n],
            send_sem=r_send.at[half, w], recv_sem=r_recv.at[half, core, 8 * yy + n],
            device_id=dev(hp - yy + lax.div(w, 16), lax.rem(lax.div(w, 8), 2), lax.rem(w, 8)),
            device_id_type=MESH)

    def dq_own(half):
        return pltpu.make_async_copy(dq_st.at[half, core], dq_out.at[:, half_cols(half, core)], d_loc.at[half])

    def dq_sib(half):
        return pltpu.make_async_remote_copy(
            src_ref=dq_st.at[half, other], dst_ref=dq_out.at[:, half_cols(half, core)],
            send_sem=d_send.at[half], recv_sem=d_recv.at[half],
            device_id=dev(hp, other, n), device_id_type=MESH)

    lax.fori_loop(0, 2, one_half, 0)

    for half in range(2):
        yy = yy_of(half)
        own = 16 * yy + 8 * core + n
        for cc in range(2):
            sum_kv[...] = jnp.zeros((2, TOK, HD), F32)

            def add(s, _):
                mine = (s == 8 * yy + n) & (core == cc)

                @pl.when((own <= 16 * lax.div(s, 8) + lax.rem(s, 8) + 8) & jnp.logical_not(mine))
                def _():
                    pltpu.make_async_remote_copy(
                        src_ref=ret.at[half, 0], dst_ref=rbuf.at[half, cc, s],
                        send_sem=r_send.at[half, 0], recv_sem=r_recv.at[half, cc, s],
                        device_id=dev(hp, core, n), device_id_type=MESH).wait_recv()
                    sum_kv[...] += rbuf[half, cc, s].astype(F32)

                @pl.when(mine)
                def _():
                    sum_kv[...] += ret[half, own].astype(F32)

                return 0

            lax.fori_loop(0, 16, add, 0)
            g = 2 * half + cc
            dk_out[:, g * HD : (g + 1) * HD] = sum_kv[0].astype(BF16)
            dv_out[:, g * HD : (g + 1) * HD] = sum_kv[1].astype(BF16)

    for half in range(2):
        for a in range(3):
            sib_copy(a, half).wait_send()
        each_gather(half, lambda copy: copy.wait_send())
        yy = yy_of(half)
        last = 16 * yy + n + 8

        def drain(w, _):
            @pl.when(w != 16 * yy + 8 * core + n)
            def _():
                return_copy(half, w, yy).wait_send()

            return 0

        lax.fori_loop(0, last + 1, drain, 0)
        dq_own(half).wait()
        dq_sib(half).wait()


def FIRST(y_lo):
    return y_lo


def body(queries, keys, values, dout, attn_out):
    nhp = lax.axis_size("outer") // 2
    anywhere = pl.BlockSpec(memory_space=pl.ANY)
    vmem = pl.BlockSpec(memory_space=pltpu.VMEM)
    dma = pltpu.SemaphoreType.DMA
    return pl.pallas_call(
        functools.partial(kernel, nhp),
        out_shape=(
            jax.ShapeDtypeStruct(queries.shape, BF16),
            jax.ShapeDtypeStruct(keys.shape, BF16),
            jax.ShapeDtypeStruct(values.shape, BF16),
        ),
        in_specs=[anywhere, vmem, vmem, anywhere, anywhere],
        out_specs=(anywhere, vmem, vmem),
        scratch_shapes=[
            pltpu.VMEM((2, 2, 2, TOK, HD), BF16),
            pltpu.VMEM((2, 32, 2, TOK, HD), BF16),
            pltpu.VMEM((2, 32, 2, TOK, HD), BF16),
            pltpu.VMEM((2, 2, 16, 2, TOK, HD), BF16),
            pltpu.VMEM((2, 2, TOK, QC), BF16),
            pltpu.VMEM((2, 2, TOK, QC), BF16),
            pltpu.VMEM((2, 2, TOK, QC), BF16),
            pltpu.VMEM((2, 2, QC, HD), BF16),
            pltpu.VMEM((2, 2, QC, HD), BF16),
            pltpu.VMEM((2, 2, 2 * HD, QC), BF16),
            pltpu.VMEM((2, 2, 2 * HD, QC), BF16),
            pltpu.VMEM((2, 2, HD, QC), F32),
            pltpu.VMEM((2, 2, TOK, QC), BF16),
            pltpu.VMEM((2, 2, 8, QC), F32),
            pltpu.VMEM((2, 2, 8, QC), F32),
            pltpu.VMEM((CK, HD), F32),
            pltpu.VMEM((CK, HD), F32),
            pltpu.VMEM((2, TOK, HD), F32),
            dma((3, 2)),
            dma((3, 2)),
            dma((3, 2)),
            dma((2, 2, 16)),
            dma((2, 32)),
            dma((2, 32)),
            dma((2, 2, 16)),
            dma((2,)),
            dma((2,)),
            dma((2,)),
        ],
        compiler_params=pltpu.CompilerParams(
            collective_id=0, has_side_effects=True, vmem_limit_bytes=56 * 2**20),
        cost_estimate=pl.CostEstimate(
            flops=12_000_000_000, bytes_accessed=6_000_000, transcendentals=16_000_000),
    )(queries, keys, values, dout, attn_out)


def solution(mesh):
    rows = P(("outer", "inner"), None)
    return jax.shard_map(
        body, mesh=mesh, in_specs=(rows,) * 5, out_specs=(rows,) * 3, check_vma=False)
```

```python
import functools

import jax
import jax.numpy as jnp
from jax import lax
from jax.experimental import pallas as pl
from jax.experimental.pallas import tpu as pltpu
from jax.sharding import PartitionSpec as P

HD = 128
REP = 8
TOK = 128
QC = REP * TOK
CH = 4
CK = CH * TOK
CB = 256
SCALE = HD**-0.5
C2 = SCALE * 1.4426950408889634
NEG = -1e30
MESH = pl.DeviceIdType.MESH
F32 = jnp.float32
BF16 = jnp.bfloat16


def split3(x):
    hi = x.astype(BF16).astype(F32)
    rest = x - hi
    mid = rest.astype(BF16).astype(F32)
    low = rest - mid
    row = lax.broadcasted_iota(jnp.int32, (HD, x.shape[1]), 0)
    out = jnp.where(row == 0, hi, jnp.where(row == 1, mid, jnp.where(row == 2, low, 0.0)))
    return out.astype(BF16)


def kernel(
    nhp,
    q_in, k_in, v_in, do_in, o_in,
    dq_out, dk_out, dv_out,
    kvpack, kvwin, ret, r1buf, rsum, r2buf, q_st, do_st, o_st, q_rows, do_rows, qt, dt, dqt, dq_st,
    m8, l8, acc_k, acc_v, sum_kv,
    x_loc, x_send, x_recv, s_send, f_send, g_recv, r1_send, r1_recv, r2_send, r2_recv, d_loc, d_send, d_recv,
):
    outer = lax.axis_index("outer")
    n = lax.axis_index("inner")
    core = lax.rem(outer, 2)
    other = 1 - core
    hp = lax.div(outer, 2)
    y_lo = lax.rem(hp, 2)
    x, yh = lax.rem(n, 4), lax.div(n, 4)
    across = lax.rem(n + 4, 8)
    heavy, light = 1 - y_lo, y_lo

    def dev(hp_, core_, n_):
        return (lax.rem(hp_ + nhp, nhp) * 2 + core_, n_)

    def half_cols(half, cc):
        return pl.ds(pl.multiple_of(half * (2 * QC) + cc * QC, QC), QC)

    def yy_of(half):
        return jnp.where(half == 0, y_lo, 1 - y_lo)

    def own_of(half):
        return 16 * yy_of(half) + 8 * core + n

    def last_of(half):
        return 16 * yy_of(half) + 8 + n

    def remote(src, dst, send, recv, to):
        return pltpu.make_async_remote_copy(
            src_ref=src, dst_ref=dst, send_sem=send, recv_sem=recv, device_id=to, device_id_type=MESH)

    sources = ((q_in, q_st), (do_in, do_st), (o_in, o_st))

    def own_copy(a, half):
        src, dst = sources[a]
        return pltpu.make_async_copy(src.at[:, half_cols(half, core)], dst.at[half, core], x_loc.at[a, half])

    def sib_copy(a, half):
        src, dst = sources[a]
        return remote(
            src.at[:, half_cols(half, other)], dst.at[half, core],
            x_send.at[a, half], x_recv.at[a, half], dev(hp, other, n))

    barrier = pltpu.get_barrier_semaphore()
    chips = [(hp, 4 * yh + lax.rem(x + t, 4)) for t in (1, 2, 3)] + [(hp, across)]
    chips += [(hp + 1, x), (hp + 1, 4 + x), (hp - 1, x), (hp - 1, 4 + x)]
    greeted = [dev(hp, other, n)] + [dev(h_, cc, n_) for h_, n_ in chips for cc in range(2)]
    for to in greeted:
        pl.semaphore_signal(barrier, inc=1, device_id=to, device_id_type=MESH)

    for a in range(3):
        for half in range(2):
            own_copy(a, half).start()
    for half in range(2):
        for cc in range(2):
            g = 2 * half + cc
            kvpack[half, cc, 0] = k_in[:, g * HD : (g + 1) * HD]
            kvpack[half, cc, 1] = v_in[:, g * HD : (g + 1) * HD]
    for half in range(2):
        for kv in range(2):
            kvwin[half, kv, own_of(half)] = kvpack[half, core, kv]

    pl.semaphore_wait(barrier, len(greeted))

    def each_source(half, kv, act):
        yy, own = yy_of(half), own_of(half)

        def send(cc, slot, to_hp, nn):
            act(remote(
                kvpack.at[half, cc, kv], kvwin.at[half, kv, own],
                s_send.at[half, kv, cc, slot], g_recv.at[half, kv, own], dev(to_hp, cc, nn)))

        for cc in range(2):
            @pl.when(core != cc)
            def _():
                send(cc, 3, hp, n)

        for t in range(3):
            send(0, t, hp, 4 * yh + lax.rem(x + 1 + t, 4))

        @pl.when(yy == 0)
        def _():
            send(1, 1, hp + 1, x)
            send(1, 2, hp + 1, 4 + x)

        send(1, 0, hp, across)

    def relay_block(half, k):
        yy = yy_of(half)
        w0 = 16 * yy + 8 * lax.div(k, 4) + 4 * yh + lax.rem(k, 4)
        w1 = 16 * (yy - lax.div(k, 4)) + 8 * lax.rem(lax.div(k, 2), 2) + 4 * lax.rem(k, 2) + x
        return jnp.where(core == 0, w0, w1), (core == 0) | (k < 4) | (yy == 1)

    def relay_peer(half, k, t):
        yy = yy_of(half)
        w, valid = relay_block(half, k)
        n1 = 4 * yh + lax.rem(x + 1 + t, 4)
        if t == 0:
            needed0 = w <= 16 * yy + 8 + across
            hp0, n0 = hp, across
        else:
            needed0 = yy == 0
            hp0, n0 = hp + 1, 4 * (t - 1) + x
        needed1 = w <= 16 * yy + 8 + n1
        to = dev(jnp.where(core == 0, hp0, hp), core, jnp.where(core == 0, n0, n1))
        return to, valid & (((core == 0) & needed0) | ((core == 1) & needed1))

    def is_relay(half, w):
        yy = yy_of(half)
        row = (lax.div(w, 16) == yy) & (lax.rem(lax.div(w, 4), 2) == yh)
        return ((core == 0) & row) | ((core == 1) & (lax.rem(w, 4) == x))

    def arrival(half, kv, w):
        return remote(
            kvpack.at[half, 0, kv], kvwin.at[half, kv, w], s_send.at[half, kv, 0, 0],
            g_recv.at[half, kv, w], dev(hp, other, n))

    def pass_on(half, kv, k, w, act):
        for t in (1, 2, 0):
            to, needed = relay_peer(half, k, t)

            @pl.when(needed)
            def _():
                block = kvwin.at[half, kv, w]
                act(remote(block, block, f_send.at[half, kv, k, t], g_recv.at[half, kv, w], to))

    def relay(half, kv):
        def one(k, _):
            w, valid = relay_block(half, k)

            @pl.when(valid & (w != own_of(half)))
            def _():
                arrival(half, kv, w).wait_recv()

            pass_on(half, kv, k, w, lambda copy: copy.start())
            return 0

        lax.fori_loop(0, 8, one, 0)

    for half in (heavy, light):
        sib_copy(0, half).start()
    for half in (heavy, light):
        each_source(half, 0, lambda copy: copy.start())
    for a in (1, 2):
        for half in (heavy, light):
            sib_copy(a, half).start()
    for half in (heavy, light):
        each_source(half, 1, lambda copy: copy.start())
    for kv in range(2):
        for half in (heavy, light):
            relay(half, kv)

    for a in range(3):
        for half in range(2):
            own_copy(a, half).wait()
            sib_copy(a, half).wait_recv()

    def prepare(i, _):
        half, b = lax.div(i, 2), lax.rem(i, 2)
        for h in range(REP):
            cols = slice(h * HD, (h + 1) * HD)
            qv = q_st[half, b, :, cols]
            dv = do_st[half, b, :, cols]
            q_rows[half, b, cols, :] = qv
            do_rows[half, b, cols, :] = dv
            qt[half, b, :HD, cols] = qv.T
            dt[half, b, :HD, cols] = dv.T
            prod = dv.astype(F32) * o_st[half, b, :, cols].astype(F32)
            delta = jnp.sum(prod.T, axis=0, keepdims=True)
            dt[half, b, HD:, cols] = split3(-delta)
        m8[half, b] = jnp.full((8, QC), NEG, F32)
        l8[half, b] = jnp.zeros((8, QC), F32)
        dqt[half, b] = jnp.zeros((HD, QC), F32)
        return 0

    lax.fori_loop(0, 4, prepare, 0)

    lane = lax.broadcasted_iota(jnp.int32, (CK, HD), 1)
    ones3 = jnp.where(lane < 3, 1.0, 0.0).astype(BF16)

    def allowed_at(j, pos):
        key = lax.broadcasted_iota(jnp.int32, (CK, CB), 0)
        tok = lax.rem(lax.broadcasted_iota(jnp.int32, (CK, CB), 1), TOK)
        return key - tok <= pos * TOK - j * CK

    def return_copy(half, w):
        yy = yy_of(half)
        same = lax.div(w, 16) == yy
        cw, yhw, xw = lax.rem(lax.div(w, 8), 2), lax.rem(lax.div(w, 4), 2), lax.rem(w, 4)
        k = jnp.where(core == 0, 4 * cw + xw, 2 * cw + yhw + jnp.where(same, 0, 4))
        t = jnp.where(core == 0, jnp.where(same, 0, 1 + yh), lax.rem(x - xw + 3, 4))
        to_hp = jnp.where((core == 0) & jnp.logical_not(same), hp - 1, hp)
        to_n = jnp.where(core == 0, 4 * yhw + x, 4 * yh + xw)
        return remote(
            ret.at[half, w], r1buf.at[half, k, t], r1_send.at[half, w], r1_recv.at[half, k, t],
            dev(to_hp, core, to_n))

    def owner_copy(half, k):
        w, _ = relay_block(half, k)
        cw, yhw, xw = lax.rem(lax.div(w, 8), 2), lax.rem(lax.div(w, 4), 2), lax.rem(w, 4)
        r = jnp.where(core == 0, x, yh + 2 * lax.div(k, 4))
        to_hp = jnp.where((core == 1) & (k >= 4), hp - 1, hp)
        return remote(
            rsum.at[half, k], r2buf.at[half, core, r], r2_send.at[half, k], r2_recv.at[half, core, r],
            dev(to_hp, cw, 4 * yhw + xw))

    def relay_sums(half):
        own, last = own_of(half), last_of(half)

        def one(k, _):
            w, valid = relay_block(half, k)

            @pl.when(valid)
            def _():
                sum_kv[...] = jnp.zeros((2, TOK, HD), F32)

                @pl.when(w <= last)
                def _():
                    sum_kv[...] = ret[half, w].astype(F32)

            for t in range(3):
                to, needed = relay_peer(half, k, t)

                @pl.when(needed)
                def _():
                    remote(
                        ret.at[half, 0], r1buf.at[half, k, t], r1_send.at[half, 0], r1_recv.at[half, k, t],
                        to).wait_recv()
                    sum_kv[...] += r1buf[half, k, t].astype(F32)

            @pl.when(valid & (w != own))
            def _():
                rsum[half, k] = sum_kv[...].astype(BF16)
                owner_copy(half, k).start()

            @pl.when(w == own)
            def _():
                r2buf[half, core, jnp.where(core == 0, x, yh)] = sum_kv[...].astype(BF16)

            return 0

        lax.fori_loop(0, 8, one, 0)

    def one_half(step, _):
        half = jnp.where(step == 0, heavy, light)
        pos0 = 16 * yy_of(half) + n
        last = pos0 + 8
        n0 = lax.div(pos0, CH) + 1
        n1 = lax.div(last, CH) + 1

        def by_mask(j, work):
            for b, count in ((1, n1), (0, n0)):
                @pl.when(j == count - 1)
                def _():
                    work(b, True)

                @pl.when(j < count - 1)
                def _():
                    work(b, False)

        def stats(i, _):
            j = n1 - 1 - i
            for u in range(CH):
                w = j * CH + u
                passed = is_relay(half, w)

                @pl.when((w <= last) & jnp.logical_not(passed))
                def _():
                    arrival(half, 0, w).wait_recv()

                @pl.when((w > last) & jnp.logical_not(passed))
                def _():
                    for kv in range(2):
                        kvwin[half, kv, w] = jnp.zeros((TOK, HD), BF16)

            def work(b, masked):
                keys = kvwin[half, 0, pl.ds(j * CH, CH)].reshape(CK, HD)
                if masked:
                    allowed = allowed_at(j, pos0 + 8 * b)
                for piece in range(QC // CB):
                    cols = slice(piece * CB, (piece + 1) * CB)
                    s = jnp.dot(keys, qt[half, b, :HD, cols], preferred_element_type=F32)
                    if masked:
                        s = jnp.where(allowed, s, NEG)
                    s = s.reshape(CK // 8, 8, CB)
                    old = m8[half, b, :, cols]
                    new = jnp.maximum(old, jnp.max(s, axis=0))
                    e = jnp.exp2((s - new[None]) * C2)
                    l8[half, b, :, cols] = l8[half, b, :, cols] * jnp.exp2((old - new) * C2) + jnp.sum(e, axis=0)
                    m8[half, b, :, cols] = new

            by_mask(j, work)
            return 0

        lax.fori_loop(0, n1, stats, 0)
        for b in range(2):
            top = jnp.max(m8[half, b], axis=0, keepdims=True)
            total = jnp.sum(l8[half, b] * jnp.exp2((m8[half, b] - top) * C2), axis=0, keepdims=True)
            qt[half, b, HD:, :] = split3(-(top + jnp.log(total) * (1.0 / SCALE)))

        @pl.when(step == 1)
        def _():
            relay_sums(heavy)

        def grads(i, _):
            j = n1 - 1 - i
            for u in range(CH):
                w = j * CH + u

                @pl.when((w <= last) & jnp.logical_not(is_relay(half, w)))
                def _():
                    arrival(half, 1, w).wait_recv()

            def work(b, masked):
                keys = kvwin[half, 0, pl.ds(j * CH, CH)].reshape(CK, HD)
                vals = kvwin[half, 1, pl.ds(j * CH, CH)].reshape(CK, HD)
                keys_t = keys.T
                keys_1 = jnp.concatenate([keys, ones3], axis=1)
                vals_1 = jnp.concatenate([vals, ones3], axis=1)
                if masked:
                    allowed = allowed_at(j, pos0 + 8 * b)
                probs, dscores = [], []
                for piece in range(QC // CB):
                    cols = slice(piece * CB, (piece + 1) * CB)
                    s = jnp.dot(keys_1, qt[half, b, :, cols], preferred_element_type=F32)
                    prob = jnp.exp2(s * C2)
                    if masked:
                        prob = jnp.where(allowed, prob, 0.0)
                    dp = jnp.dot(vals_1, dt[half, b, :, cols], preferred_element_type=F32)
                    ds = (prob * dp).astype(BF16)
                    dqt[half, b, :, cols] += jnp.dot(keys_t, ds, preferred_element_type=F32)
                    probs.append(prob.astype(BF16))
                    dscores.append(ds)
                dv = jnp.dot(jnp.concatenate(probs, axis=1), do_rows[half, b], preferred_element_type=F32)
                dk = jnp.dot(jnp.concatenate(dscores, axis=1), q_rows[half, b], preferred_element_type=F32)
                if b == 1:
                    acc_k[...] = dk
                    acc_v[...] = dv
                else:
                    acc_k[...] += dk
                    acc_v[...] += dv

            by_mask(j, work)
            for u in range(CH):
                w = j * CH + u

                @pl.when(w <= last)
                def _():
                    rows = slice(u * TOK, (u + 1) * TOK)
                    ret[half, w, 0] = (acc_k[rows] * SCALE).astype(BF16)
                    ret[half, w, 1] = acc_v[rows].astype(BF16)

                    @pl.when(jnp.logical_not(is_relay(half, w)))
                    def _():
                        return_copy(half, w).start()

            return 0

        lax.fori_loop(0, n1, grads, 0)

        for b in range(2):
            for h in range(REP):
                cols = slice(h * HD, (h + 1) * HD)
                dq_st[half, b, :, cols] = (dqt[half, b, :, cols] * SCALE).T.astype(BF16)
        dq_own(half).start()
        dq_sib(half).start()
        return 0

    def dq_own(half):
        return pltpu.make_async_copy(dq_st.at[half, core], dq_out.at[:, half_cols(half, core)], d_loc.at[half])

    def dq_sib(half):
        return remote(
            dq_st.at[half, other], dq_out.at[:, half_cols(half, core)], d_send.at[half], d_recv.at[half],
            dev(hp, other, n))

    lax.fori_loop(0, 2, one_half, 0)
    relay_sums(light)

    for half in range(2):
        for cc in range(2):
            sum_kv[...] = jnp.zeros((2, TOK, HD), F32)
            for r in range(4):
                mine = (core == cc) & (r == jnp.where(core == 0, x, yh))
                there = (cc == 0) | (r < 2) | (yy_of(half) == 0)

                @pl.when(there & jnp.logical_not(mine))
                def _():
                    remote(
                        rsum.at[half, 0], r2buf.at[half, cc, r], r2_send.at[half, 0], r2_recv.at[half, cc, r],
                        dev(hp, other, n)).wait_recv()

                @pl.when(there)
                def _():
                    sum_kv[...] += r2buf[half, cc, r].astype(F32)

            g = 2 * half + cc
            dk_out[:, g * HD : (g + 1) * HD] = sum_kv[0].astype(BF16)
            dv_out[:, g * HD : (g + 1) * HD] = sum_kv[1].astype(BF16)

    for half in range(2):
        for a in range(3):
            sib_copy(a, half).wait_send()
        for kv in range(2):
            each_source(half, kv, lambda copy: copy.wait_send())

        def drain_relay(k, _):
            w, valid = relay_block(half, k)
            for kv in range(2):
                pass_on(half, kv, k, w, lambda copy: copy.wait_send())

            @pl.when(valid & (w != own_of(half)))
            def _():
                owner_copy(half, k).wait_send()

            return 0

        lax.fori_loop(0, 8, drain_relay, 0)

        def drain(w, _):
            @pl.when(jnp.logical_not(is_relay(half, w)))
            def _():
                return_copy(half, w).wait_send()

            return 0

        lax.fori_loop(0, last_of(half) + 1, drain, 0)
        dq_own(half).wait()
        dq_sib(half).wait()


def body(queries, keys, values, dout, attn_out):
    nhp = lax.axis_size("outer") // 2
    anywhere = pl.BlockSpec(memory_space=pl.ANY)
    vmem = pl.BlockSpec(memory_space=pltpu.VMEM)
    dma = pltpu.SemaphoreType.DMA
    return pl.pallas_call(
        functools.partial(kernel, nhp),
        out_shape=(
            jax.ShapeDtypeStruct(queries.shape, BF16),
            jax.ShapeDtypeStruct(keys.shape, BF16),
            jax.ShapeDtypeStruct(values.shape, BF16),
        ),
        in_specs=[anywhere, vmem, vmem, anywhere, anywhere],
        out_specs=(anywhere, vmem, vmem),
        scratch_shapes=[
            pltpu.VMEM((2, 2, 2, TOK, HD), BF16),
            pltpu.VMEM((2, 2, 32, TOK, HD), BF16),
            pltpu.VMEM((2, 32, 2, TOK, HD), BF16),
            pltpu.VMEM((2, 8, 3, 2, TOK, HD), BF16),
            pltpu.VMEM((2, 8, 2, TOK, HD), BF16),
            pltpu.VMEM((2, 2, 4, 2, TOK, HD), BF16),
            pltpu.VMEM((2, 2, TOK, QC), BF16),
            pltpu.VMEM((2, 2, TOK, QC), BF16),
            pltpu.VMEM((2, 2, TOK, QC), BF16),
            pltpu.VMEM((2, 2, QC, HD), BF16),
            pltpu.VMEM((2, 2, QC, HD), BF16),
            pltpu.VMEM((2, 2, 2 * HD, QC), BF16),
            pltpu.VMEM((2, 2, 2 * HD, QC), BF16),
            pltpu.VMEM((2, 2, HD, QC), F32),
            pltpu.VMEM((2, 2, TOK, QC), BF16),
            pltpu.VMEM((2, 2, 8, QC), F32),
            pltpu.VMEM((2, 2, 8, QC), F32),
            pltpu.VMEM((CK, HD), F32),
            pltpu.VMEM((CK, HD), F32),
            pltpu.VMEM((2, TOK, HD), F32),
            dma((3, 2)),
            dma((3, 2)),
            dma((3, 2)),
            dma((2, 2, 2, 4)),
            dma((2, 2, 8, 3)),
            dma((2, 2, 32)),
            dma((2, 32)),
            dma((2, 8, 3)),
            dma((2, 8)),
            dma((2, 2, 4)),
            dma((2,)),
            dma((2,)),
            dma((2,)),
        ],
        compiler_params=pltpu.CompilerParams(
            collective_id=0, has_side_effects=True, vmem_limit_bytes=56 * 2**20),
        cost_estimate=pl.CostEstimate(
            flops=12_000_000_000, bytes_accessed=6_000_000, transcendentals=16_000_000),
    )(queries, keys, values, dout, attn_out)


def solution(mesh):
    rows = P(("outer", "inner"), None)
    return jax.shard_map(
        body, mesh=mesh, in_specs=(rows,) * 5, out_specs=(rows,) * 3, check_vma=False)
```

```python
import functools

import jax
import jax.numpy as jnp
from jax import lax
from jax.experimental import pallas as pl
from jax.experimental.pallas import tpu as pltpu
from jax.sharding import PartitionSpec as P

HD = 128
REP = 8
TOK = 128
QC = REP * TOK
CH = 8
CK = CH * TOK
CB = 256
SCALE = HD**-0.5
C2 = SCALE * 1.4426950408889634
NEG = -1e30
MESH = pl.DeviceIdType.MESH
F32 = jnp.float32
BF16 = jnp.bfloat16


def split3(x):
    hi = x.astype(BF16).astype(F32)
    rest = x - hi
    mid = rest.astype(BF16).astype(F32)
    low = rest - mid
    row = lax.broadcasted_iota(jnp.int32, (HD, x.shape[1]), 0)
    out = jnp.where(row == 0, hi, jnp.where(row == 1, mid, jnp.where(row == 2, low, 0.0)))
    return out.astype(BF16)


def kernel(
    nhp,
    q_in, k_in, v_in, do_in, o_in,
    dq_out, dk_out, dv_out,
    kvpack, kvwin, ret, r1buf, rsum, r2buf, q_st, do_st, o_st, q_rows, do_rows, qt, dt, dqt, dq_st,
    m8, l8, probs, dscores, acc_k, acc_v, sum_kv,
    x_loc, x_send, x_recv, s_send, f_send, g_recv, r1_send, r1_recv, r2_send, r2_recv, d_loc, d_send, d_recv,
):
    outer = lax.axis_index("outer")
    n = lax.axis_index("inner")
    core = lax.rem(outer, 2)
    other = 1 - core
    hp = lax.div(outer, 2)
    y_lo = lax.rem(hp, 2)
    x, yh = lax.rem(n, 4), lax.div(n, 4)
    across = lax.rem(n + 4, 8)
    heavy, light = 1 - y_lo, y_lo

    def dev(hp_, core_, n_):
        return (lax.rem(hp_ + nhp, nhp) * 2 + core_, n_)

    def half_cols(half, cc):
        return pl.ds(pl.multiple_of(half * (2 * QC) + cc * QC, QC), QC)

    def yy_of(half):
        return jnp.where(half == 0, y_lo, 1 - y_lo)

    def own_of(half):
        return 16 * yy_of(half) + 8 * core + n

    def last_of(half):
        return 16 * yy_of(half) + 8 + n

    def remote(src, dst, send, recv, to):
        return pltpu.make_async_remote_copy(
            src_ref=src, dst_ref=dst, send_sem=send, recv_sem=recv, device_id=to, device_id_type=MESH)

    sources = ((q_in, q_st), (do_in, do_st), (o_in, o_st))

    def own_copy(a, half):
        src, dst = sources[a]
        return pltpu.make_async_copy(src.at[:, half_cols(half, core)], dst.at[half, core], x_loc.at[a, half])

    def sib_copy(a, half):
        src, dst = sources[a]
        return remote(
            src.at[:, half_cols(half, other)], dst.at[half, core],
            x_send.at[a, half], x_recv.at[a, half], dev(hp, other, n))

    barrier = pltpu.get_barrier_semaphore()
    chips = [(hp, 4 * yh + lax.rem(x + t, 4)) for t in (1, 2, 3)] + [(hp, across)]
    chips += [(hp + 1, x), (hp + 1, 4 + x), (hp - 1, x), (hp - 1, 4 + x)]
    greeted = [dev(hp, other, n)] + [dev(h_, cc, n_) for h_, n_ in chips for cc in range(2)]
    for to in greeted:
        pl.semaphore_signal(barrier, inc=1, device_id=to, device_id_type=MESH)

    for a in range(3):
        for half in range(2):
            own_copy(a, half).start()
    for half in range(2):
        for cc in range(2):
            g = 2 * half + cc
            kvpack[half, cc, 0] = k_in[:, g * HD : (g + 1) * HD]
            kvpack[half, cc, 1] = v_in[:, g * HD : (g + 1) * HD]
    for half in range(2):
        for kv in range(2):
            kvwin[half, kv, own_of(half)] = kvpack[half, core, kv]

    pl.semaphore_wait(barrier, len(greeted))

    def each_source(half, kv, act):
        yy, own = yy_of(half), own_of(half)

        def send(cc, slot, to_hp, nn):
            act(remote(
                kvpack.at[half, cc, kv], kvwin.at[half, kv, own],
                s_send.at[half, kv, cc, slot], g_recv.at[half, kv, own], dev(to_hp, cc, nn)))

        for cc in range(2):
            @pl.when(core != cc)
            def _():
                send(cc, 3, hp, n)

        for t in range(3):
            send(0, t, hp, 4 * yh + lax.rem(x + 1 + t, 4))

        @pl.when(yy == 0)
        def _():
            send(1, 1, hp + 1, x)
            send(1, 2, hp + 1, 4 + x)

        send(1, 0, hp, across)

    def relay_block(half, k):
        yy = yy_of(half)
        w0 = 16 * yy + 8 * lax.div(k, 4) + 4 * yh + lax.rem(k, 4)
        w1 = 16 * (yy - lax.div(k, 4)) + 8 * lax.rem(lax.div(k, 2), 2) + 4 * lax.rem(k, 2) + x
        return jnp.where(core == 0, w0, w1), (core == 0) | (k < 4) | (yy == 1)

    def relay_peer(half, k, t):
        yy = yy_of(half)
        w, valid = relay_block(half, k)
        n1 = 4 * yh + lax.rem(x + 1 + t, 4)
        if t == 0:
            needed0 = w <= 16 * yy + 8 + across
            hp0, n0 = hp, across
        else:
            needed0 = yy == 0
            hp0, n0 = hp + 1, 4 * (t - 1) + x
        needed1 = w <= 16 * yy + 8 + n1
        to = dev(jnp.where(core == 0, hp0, hp), core, jnp.where(core == 0, n0, n1))
        return to, valid & (((core == 0) & needed0) | ((core == 1) & needed1))

    def is_relay(half, w):
        yy = yy_of(half)
        row = (lax.div(w, 16) == yy) & (lax.rem(lax.div(w, 4), 2) == yh)
        return ((core == 0) & row) | ((core == 1) & (lax.rem(w, 4) == x))

    def arrival(half, kv, w):
        return remote(
            kvpack.at[half, 0, kv], kvwin.at[half, kv, w], s_send.at[half, kv, 0, 0],
            g_recv.at[half, kv, w], dev(hp, other, n))

    def pass_on(half, kv, k, w, act):
        for t in (1, 2, 0):
            to, needed = relay_peer(half, k, t)

            @pl.when(needed)
            def _():
                block = kvwin.at[half, kv, w]
                act(remote(block, block, f_send.at[half, kv, k, t], g_recv.at[half, kv, w], to))

    def relay(half, kv):
        def one(k, _):
            w, valid = relay_block(half, k)

            @pl.when(valid & (w != own_of(half)))
            def _():
                arrival(half, kv, w).wait_recv()

            pass_on(half, kv, k, w, lambda copy: copy.start())
            return 0

        lax.fori_loop(0, 8, one, 0)

    for half in (heavy, light):
        sib_copy(0, half).start()
    for half in (heavy, light):
        each_source(half, 0, lambda copy: copy.start())
    for a in (1, 2):
        for half in (heavy, light):
            sib_copy(a, half).start()
    for half in (heavy, light):
        each_source(half, 1, lambda copy: copy.start())
    for half in (heavy, light):
        relay(half, 0)

    def landed(a):
        for half in range(2):
            own_copy(a, half).wait()
            sib_copy(a, half).wait_recv()

    def prepare_q(half, _):
        for b in range(2):
            for h in range(REP):
                qv = q_st[half, b, :, h * HD : (h + 1) * HD]
                cols = slice(b * QC + h * HD, b * QC + (h + 1) * HD)
                q_rows[half, cols, :] = qv
                qt[half, :HD, cols] = qv.T
        m8[half] = jnp.full((8, 2 * QC), NEG, F32)
        l8[half] = jnp.zeros((8, 2 * QC), F32)
        dqt[half] = jnp.zeros((HD, 2 * QC), F32)
        return 0

    def prepare_d(half, _):
        for b in range(2):
            for h in range(REP):
                dv = do_st[half, b, :, h * HD : (h + 1) * HD]
                ov = o_st[half, b, :, h * HD : (h + 1) * HD]
                cols = slice(b * QC + h * HD, b * QC + (h + 1) * HD)
                do_rows[half, cols, :] = dv
                dt[half, :HD, cols] = dv.T
                prod = dv.astype(F32) * ov.astype(F32)
                dt[half, HD:, cols] = split3(-jnp.sum(prod.T, axis=0, keepdims=True))
        return 0

    landed(0)
    lax.fori_loop(0, 2, prepare_q, 0)
    for half in (heavy, light):
        relay(half, 1)
    landed(1)
    landed(2)
    lax.fori_loop(0, 2, prepare_d, 0)

    lane = lax.broadcasted_iota(jnp.int32, (CK, HD), 1)
    ones3 = jnp.where(lane < 3, 1.0, 0.0).astype(BF16)

    def allowed_at():
        key = lax.broadcasted_iota(jnp.int32, (CK, CB), 0)
        tok = lax.rem(lax.broadcasted_iota(jnp.int32, (CK, CB), 1), TOK)
        return key - tok <= n * TOK

    def return_copy(half, w):
        yy = yy_of(half)
        same = lax.div(w, 16) == yy
        cw, yhw, xw = lax.rem(lax.div(w, 8), 2), lax.rem(lax.div(w, 4), 2), lax.rem(w, 4)
        k = jnp.where(core == 0, 4 * cw + xw, 2 * cw + yhw + jnp.where(same, 0, 4))
        t = jnp.where(core == 0, jnp.where(same, 0, 1 + yh), lax.rem(x - xw + 3, 4))
        to_hp = jnp.where((core == 0) & jnp.logical_not(same), hp - 1, hp)
        to_n = jnp.where(core == 0, 4 * yhw + x, 4 * yh + xw)
        return remote(
            ret.at[half, w], r1buf.at[half, k, t], r1_send.at[half, w], r1_recv.at[half, k, t],
            dev(to_hp, core, to_n))

    def owner_copy(half, k):
        w, _ = relay_block(half, k)
        cw, yhw, xw = lax.rem(lax.div(w, 8), 2), lax.rem(lax.div(w, 4), 2), lax.rem(w, 4)
        r = jnp.where(core == 0, x, yh + 2 * lax.div(k, 4))
        to_hp = jnp.where((core == 1) & (k >= 4), hp - 1, hp)
        return remote(
            rsum.at[half, k], r2buf.at[half, core, r], r2_send.at[half, k], r2_recv.at[half, core, r],
            dev(to_hp, cw, 4 * yhw + xw))

    def relay_sums(half):
        own, last = own_of(half), last_of(half)

        def one(k, _):
            w, valid = relay_block(half, k)

            @pl.when(valid)
            def _():
                sum_kv[...] = jnp.zeros((2, TOK, HD), F32)

                @pl.when(w <= last)
                def _():
                    sum_kv[...] = ret[half, w].astype(F32)

            for t in range(3):
                to, needed = relay_peer(half, k, t)

                @pl.when(needed)
                def _():
                    remote(
                        ret.at[half, 0], r1buf.at[half, k, t], r1_send.at[half, 0], r1_recv.at[half, k, t],
                        to).wait_recv()
                    sum_kv[...] += r1buf[half, k, t].astype(F32)

            @pl.when(valid & (w != own))
            def _():
                rsum[half, k] = sum_kv[...].astype(BF16)
                owner_copy(half, k).start()

            @pl.when(w == own)
            def _():
                r2buf[half, core, jnp.where(core == 0, x, yh)] = sum_kv[...].astype(BF16)

            return 0

        lax.fori_loop(0, 8, one, 0)

    def one_half(step, _):
        half = jnp.where(step == 0, heavy, light)
        pos0 = 16 * yy_of(half) + n
        last = pos0 + 8
        n1 = lax.div(last, CH) + 1

        def by_mask(j, work):
            half_cols = QC // CB

            @pl.when(j == n1 - 1)
            def _():
                work(range(half_cols, 2 * half_cols), range(half_cols, 2 * half_cols))

            @pl.when(j == n1 - 2)
            def _():
                work(range(2 * half_cols), range(half_cols))

            @pl.when(j < n1 - 2)
            def _():
                work(range(2 * half_cols), ())

        def stats(i, _):
            j = n1 - 1 - i
            for u in range(CH):
                w = j * CH + u
                passed = is_relay(half, w)

                @pl.when((w <= last) & jnp.logical_not(passed))
                def _():
                    arrival(half, 0, w).wait_recv()

                @pl.when((w > last) & jnp.logical_not(passed))
                def _():
                    for kv in range(2):
                        kvwin[half, kv, w] = jnp.zeros((TOK, HD), BF16)

            def work(pieces, masked):
                keys = kvwin[half, 0, pl.ds(j * CH, CH)].reshape(CK, HD)
                for piece in pieces:
                    cols = slice(piece * CB, (piece + 1) * CB)
                    s = jnp.dot(keys, qt[half, :HD, cols], preferred_element_type=F32)
                    if piece in masked:
                        s = jnp.where(allowed_at(), s, NEG)
                    s = s.reshape(CK // 8, 8, CB)
                    old = m8[half, :, cols]
                    new = jnp.maximum(old, jnp.max(s, axis=0))
                    e = jnp.exp2((s - new[None]) * C2)
                    l8[half, :, cols] = l8[half, :, cols] * jnp.exp2((old - new) * C2) + jnp.sum(e, axis=0)
                    m8[half, :, cols] = new

            by_mask(j, work)
            return 0

        lax.fori_loop(0, n1, stats, 0)
        top = jnp.max(m8[half], axis=0, keepdims=True)
        total = jnp.sum(l8[half] * jnp.exp2((m8[half] - top) * C2), axis=0, keepdims=True)
        qt[half, HD:, :] = split3(-(top + jnp.log(total) * (1.0 / SCALE)))

        @pl.when(step == 1)
        def _():
            relay_sums(heavy)

        def grads(i, _):
            j = n1 - 1 - i
            for u in range(CH):
                w = j * CH + u

                @pl.when((w <= last) & jnp.logical_not(is_relay(half, w)))
                def _():
                    arrival(half, 1, w).wait_recv()

            def work(pieces, masked):
                keys = kvwin[half, 0, pl.ds(j * CH, CH)].reshape(CK, HD)
                vals = kvwin[half, 1, pl.ds(j * CH, CH)].reshape(CK, HD)
                keys_t = keys.T
                keys_1 = jnp.concatenate([keys, ones3], axis=1)
                vals_1 = jnp.concatenate([vals, ones3], axis=1)
                for piece in pieces:
                    cols = slice(piece * CB, (piece + 1) * CB)
                    s = jnp.dot(keys_1, qt[half, :, cols], preferred_element_type=F32)
                    prob = jnp.exp2(s * C2)
                    if piece in masked:
                        prob = jnp.where(allowed_at(), prob, 0.0)
                    dp = jnp.dot(vals_1, dt[half, :, cols], preferred_element_type=F32)
                    probs[:, cols] = prob.astype(BF16)
                    dscores[:, cols] = (prob * dp).astype(BF16)
                both = slice(pieces[0] * CB, (pieces[-1] + 1) * CB)
                acc_v[...] = jnp.dot(probs[:, both], do_rows[half, both, :], preferred_element_type=F32)
                acc_k[...] = jnp.dot(dscores[:, both], q_rows[half, both, :], preferred_element_type=F32)
                dqt[half, :, both] += jnp.dot(keys_t, dscores[:, both], preferred_element_type=F32)

            by_mask(j, work)
            for u in range(CH):
                w = j * CH + u

                @pl.when(w <= last)
                def _():
                    rows = slice(u * TOK, (u + 1) * TOK)
                    ret[half, w, 0] = (acc_k[rows] * SCALE).astype(BF16)
                    ret[half, w, 1] = acc_v[rows].astype(BF16)

                    @pl.when(jnp.logical_not(is_relay(half, w)))
                    def _():
                        return_copy(half, w).start()

            return 0

        lax.fori_loop(0, n1, grads, 0)

        for b in range(2):
            for h in range(REP):
                cols = slice(h * HD, (h + 1) * HD)
                mine = slice(b * QC + h * HD, b * QC + (h + 1) * HD)
                dq_st[half, b, :, cols] = (dqt[half, :, mine] * SCALE).T.astype(BF16)
        dq_own(half).start()
        dq_sib(half).start()
        return 0

    def dq_own(half):
        return pltpu.make_async_copy(dq_st.at[half, core], dq_out.at[:, half_cols(half, core)], d_loc.at[half])

    def dq_sib(half):
        return remote(
            dq_st.at[half, other], dq_out.at[:, half_cols(half, core)], d_send.at[half], d_recv.at[half],
            dev(hp, other, n))

    lax.fori_loop(0, 2, one_half, 0)
    relay_sums(light)

    for half in range(2):
        for cc in range(2):
            sum_kv[...] = jnp.zeros((2, TOK, HD), F32)
            for r in range(4):
                mine = (core == cc) & (r == jnp.where(core == 0, x, yh))
                there = (cc == 0) | (r < 2) | (yy_of(half) == 0)

                @pl.when(there & jnp.logical_not(mine))
                def _():
                    remote(
                        rsum.at[half, 0], r2buf.at[half, cc, r], r2_send.at[half, 0], r2_recv.at[half, cc, r],
                        dev(hp, other, n)).wait_recv()

                @pl.when(there)
                def _():
                    sum_kv[...] += r2buf[half, cc, r].astype(F32)

            g = 2 * half + cc
            dk_out[:, g * HD : (g + 1) * HD] = sum_kv[0].astype(BF16)
            dv_out[:, g * HD : (g + 1) * HD] = sum_kv[1].astype(BF16)

    for half in range(2):
        for a in range(3):
            sib_copy(a, half).wait_send()
        for kv in range(2):
            each_source(half, kv, lambda copy: copy.wait_send())

        def drain_relay(k, _):
            w, valid = relay_block(half, k)
            for kv in range(2):
                pass_on(half, kv, k, w, lambda copy: copy.wait_send())

            @pl.when(valid & (w != own_of(half)))
            def _():
                owner_copy(half, k).wait_send()

            return 0

        lax.fori_loop(0, 8, drain_relay, 0)

        def drain(w, _):
            @pl.when(jnp.logical_not(is_relay(half, w)))
            def _():
                return_copy(half, w).wait_send()

            return 0

        lax.fori_loop(0, last_of(half) + 1, drain, 0)
        dq_own(half).wait()
        dq_sib(half).wait()


def body(queries, keys, values, dout, attn_out):
    nhp = lax.axis_size("outer") // 2
    anywhere = pl.BlockSpec(memory_space=pl.ANY)
    vmem = pl.BlockSpec(memory_space=pltpu.VMEM)
    dma = pltpu.SemaphoreType.DMA
    return pl.pallas_call(
        functools.partial(kernel, nhp),
        out_shape=(
            jax.ShapeDtypeStruct(queries.shape, BF16),
            jax.ShapeDtypeStruct(keys.shape, BF16),
            jax.ShapeDtypeStruct(values.shape, BF16),
        ),
        in_specs=[anywhere, vmem, vmem, anywhere, anywhere],
        out_specs=(anywhere, vmem, vmem),
        scratch_shapes=[
            pltpu.VMEM((2, 2, 2, TOK, HD), BF16),
            pltpu.VMEM((2, 2, 32, TOK, HD), BF16),
            pltpu.VMEM((2, 32, 2, TOK, HD), BF16),
            pltpu.VMEM((2, 8, 3, 2, TOK, HD), BF16),
            pltpu.VMEM((2, 8, 2, TOK, HD), BF16),
            pltpu.VMEM((2, 2, 4, 2, TOK, HD), BF16),
            pltpu.VMEM((2, 2, TOK, QC), BF16),
            pltpu.VMEM((2, 2, TOK, QC), BF16),
            pltpu.VMEM((2, 2, TOK, QC), BF16),
            pltpu.VMEM((2, 2 * QC, HD), BF16),
            pltpu.VMEM((2, 2 * QC, HD), BF16),
            pltpu.VMEM((2, 2 * HD, 2 * QC), BF16),
            pltpu.VMEM((2, 2 * HD, 2 * QC), BF16),
            pltpu.VMEM((2, HD, 2 * QC), F32),
            pltpu.VMEM((2, 2, TOK, QC), BF16),
            pltpu.VMEM((2, 8, 2 * QC), F32),
            pltpu.VMEM((2, 8, 2 * QC), F32),
            pltpu.VMEM((CK, 2 * QC), BF16),
            pltpu.VMEM((CK, 2 * QC), BF16),
            pltpu.VMEM((CK, HD), F32),
            pltpu.VMEM((CK, HD), F32),
            pltpu.VMEM((2, TOK, HD), F32),
            dma((3, 2)),
            dma((3, 2)),
            dma((3, 2)),
            dma((2, 2, 2, 4)),
            dma((2, 2, 8, 3)),
            dma((2, 2, 32)),
            dma((2, 32)),
            dma((2, 8, 3)),
            dma((2, 8)),
            dma((2, 2, 4)),
            dma((2,)),
            dma((2,)),
            dma((2,)),
        ],
        compiler_params=pltpu.CompilerParams(
            collective_id=0, has_side_effects=True, vmem_limit_bytes=56 * 2**20),
        cost_estimate=pl.CostEstimate(
            flops=12_000_000_000, bytes_accessed=6_000_000, transcendentals=16_000_000),
    )(queries, keys, values, dout, attn_out)


def solution(mesh):
    rows = P(("outer", "inner"), None)
    return jax.shard_map(
        body, mesh=mesh, in_specs=(rows,) * 5, out_specs=(rows,) * 3, check_vma=False)
```

```python
import functools

import jax
import jax.numpy as jnp
from jax import lax
from jax.experimental import pallas as pl
from jax.experimental.pallas import tpu as pltpu
from jax.sharding import PartitionSpec as P

HD = 128
REP = 8
TOK = 128
QC = REP * TOK
CH = 8
CK = CH * TOK
CB = 256
SCALE = HD**-0.5
C2 = SCALE * 1.4426950408889634
NEG = -1e30
MESH = pl.DeviceIdType.MESH
F32 = jnp.float32
BF16 = jnp.bfloat16


def split3(x):
    hi = x.astype(BF16).astype(F32)
    rest = x - hi
    mid = rest.astype(BF16).astype(F32)
    low = rest - mid
    row = lax.broadcasted_iota(jnp.int32, (HD, x.shape[1]), 0)
    out = jnp.where(row == 0, hi, jnp.where(row == 1, mid, jnp.where(row == 2, low, 0.0)))
    return out.astype(BF16)


def kernel(
    nhp,
    q_in, k_in, v_in, do_in, o_in,
    dq_out, dk_out, dv_out,
    kvpack, kvwin, ret, r1buf, rsum, r2buf, q_st, do_st, o_st, q_rows, do_rows, qt, dt, dqt, dq_st,
    m8, l8, m_at, probs, dscores, acc_k, acc_v, sum_kv,
    x_loc, x_send, x_recv, s_send, f_send, g_recv, r1_send, r1_recv, r2_send, r2_recv, d_loc, d_send, d_recv,
):
    outer = lax.axis_index("outer")
    n = lax.axis_index("inner")
    core = lax.rem(outer, 2)
    other = 1 - core
    hp = lax.div(outer, 2)
    y_lo = lax.rem(hp, 2)
    x, yh = lax.rem(n, 4), lax.div(n, 4)
    across = lax.rem(n + 4, 8)
    heavy, light = 1 - y_lo, y_lo

    def dev(hp_, core_, n_):
        return (lax.rem(hp_ + nhp, nhp) * 2 + core_, n_)

    def half_cols(half, cc):
        return pl.ds(pl.multiple_of(half * (2 * QC) + cc * QC, QC), QC)

    def yy_of(half):
        return jnp.where(half == 0, y_lo, 1 - y_lo)

    def own_of(half):
        return 16 * yy_of(half) + 8 * core + n

    def last_of(half):
        return 16 * yy_of(half) + 8 + n

    def remote(src, dst, send, recv, to):
        return pltpu.make_async_remote_copy(
            src_ref=src, dst_ref=dst, send_sem=send, recv_sem=recv, device_id=to, device_id_type=MESH)

    sources = ((q_in, q_st), (do_in, do_st), (o_in, o_st))

    def own_copy(a, half):
        src, dst = sources[a]
        return pltpu.make_async_copy(src.at[:, half_cols(half, core)], dst.at[half, core], x_loc.at[a, half])

    def sib_copy(a, half):
        src, dst = sources[a]
        return remote(
            src.at[:, half_cols(half, other)], dst.at[half, core],
            x_send.at[a, half], x_recv.at[a, half], dev(hp, other, n))

    barrier = pltpu.get_barrier_semaphore()
    chips = [(hp, 4 * yh + lax.rem(x + t, 4)) for t in (1, 2, 3)] + [(hp, across)]
    chips += [(hp + 1, x), (hp + 1, 4 + x), (hp - 1, x), (hp - 1, 4 + x)]
    greeted = [dev(hp, other, n)] + [dev(h_, cc, n_) for h_, n_ in chips for cc in range(2)]
    for to in greeted:
        pl.semaphore_signal(barrier, inc=1, device_id=to, device_id_type=MESH)

    for a in range(3):
        for half in range(2):
            own_copy(a, half).start()
    for half in range(2):
        for cc in range(2):
            g = 2 * half + cc
            kvpack[half, cc, 0] = k_in[:, g * HD : (g + 1) * HD]
            kvpack[half, cc, 1] = v_in[:, g * HD : (g + 1) * HD]
    for half in range(2):
        for kv in range(2):
            kvwin[half, kv, own_of(half)] = kvpack[half, core, kv]

    pl.semaphore_wait(barrier, len(greeted))

    def each_source(half, kv, late, act):
        yy, own = yy_of(half), own_of(half)

        def send(cc, slot, to_hp, nn):
            act(remote(
                kvpack.at[half, cc, kv], kvwin.at[half, kv, own],
                s_send.at[half, kv, cc, slot], g_recv.at[half, kv, own], dev(to_hp, cc, nn)))

        if not late:
            for cc in range(2):
                @pl.when(core != cc)
                def _():
                    send(cc, 3, hp, n)

            for t in range(3):
                send(0, t, hp, 4 * yh + lax.rem(x + 1 + t, 4))

            @pl.when(yy == 0)
            def _():
                send(1, 1, hp + 1, x)
                send(1, 2, hp + 1, 4 + x)

        @pl.when(yy == (0 if late else 1))
        def _():
            send(1, 0, hp, across)

    def relay_block(half, k):
        yy = yy_of(half)
        w0 = 16 * yy + 8 * lax.div(k, 4) + 4 * yh + lax.rem(k, 4)
        w1 = 16 * (yy - lax.div(k, 4)) + 8 * lax.rem(lax.div(k, 2), 2) + 4 * lax.rem(k, 2) + x
        return jnp.where(core == 0, w0, w1), (core == 0) | (k < 4) | (yy == 1)

    def relay_peer(half, k, t):
        yy = yy_of(half)
        w, valid = relay_block(half, k)
        n1 = 4 * yh + lax.rem(x + 1 + t, 4)
        if t == 0:
            needed0 = w <= 16 * yy + 8 + across
            hp0, n0 = hp, across
        else:
            needed0 = yy == 0
            hp0, n0 = hp + 1, 4 * (t - 1) + x
        needed1 = w <= 16 * yy + 8 + n1
        to = dev(jnp.where(core == 0, hp0, hp), core, jnp.where(core == 0, n0, n1))
        return to, valid & (((core == 0) & needed0) | ((core == 1) & needed1))

    def is_relay(half, w):
        yy = yy_of(half)
        row = (lax.div(w, 16) == yy) & (lax.rem(lax.div(w, 4), 2) == yh)
        return ((core == 0) & row) | ((core == 1) & (lax.rem(w, 4) == x))

    def arrival(half, kv, w):
        return remote(
            kvpack.at[half, 0, kv], kvwin.at[half, kv, w], s_send.at[half, kv, 0, 0],
            g_recv.at[half, kv, w], dev(hp, other, n))

    def pass_on(half, kv, k, w, peers, act):
        for t in peers:
            to, needed = relay_peer(half, k, t)

            @pl.when(needed)
            def _():
                block = kvwin.at[half, kv, w]
                act(remote(block, block, f_send.at[half, kv, k, t], g_recv.at[half, kv, w], to))

    def relay(half, kv, part):
        def one(k, _):
            w, valid = relay_block(half, k)

            @pl.when(valid & (w != own_of(half)))
            def _():
                arrival(half, kv, w).wait_recv()

            pass_on(half, kv, k, w, (0, 1, 2) if part == 0 else (1, 2), lambda copy: copy.start())
            return 0

        def again(k, _):
            w, _ = relay_block(half, k)
            pass_on(half, kv, k, w, (0,), lambda copy: copy.start())
            return 0

        if part == 0:
            lax.fori_loop(0, 8, one, 0)
        elif part == 1:
            @pl.when(core == 0)
            def _():
                lax.fori_loop(0, 8, one, 0)
        else:
            @pl.when(core == 0)
            def _():
                lax.fori_loop(0, 8, again, 0)

            @pl.when(core == 1)
            def _():
                def column(k, _):
                    w, valid = relay_block(half, k)

                    @pl.when(valid & (w != own_of(half)))
                    def _():
                        arrival(half, kv, w).wait_recv()

                    pass_on(half, kv, k, w, (0, 1, 2), lambda copy: copy.start())
                    return 0

                lax.fori_loop(0, 8, column, 0)

    start = lambda copy: copy.start()
    for half in (heavy, light):
        sib_copy(0, half).start()
    for kv in range(2):
        for half in (heavy, light):
            each_source(half, kv, False, start)
    for kv in range(2):
        each_source(light, kv, True, start)
    for a in (1, 2):
        for half in (heavy, light):
            sib_copy(a, half).start()

    def prepare_q(half, b):
        for h in range(REP):
            qv = q_st[half, b, :, h * HD : (h + 1) * HD]
            cols = pl.ds(pl.multiple_of(b * QC + h * HD, HD), HD)
            q_rows[half, cols, :] = qv
            qt[half, :, cols] = qv.T

    def prepare_d(half, _):
        for b in range(2):
            for h in range(REP):
                dv = do_st[half, b, :, h * HD : (h + 1) * HD]
                ov = o_st[half, b, :, h * HD : (h + 1) * HD]
                cols = slice(b * QC + h * HD, b * QC + (h + 1) * HD)
                do_rows[half, cols, :] = dv
                dt[half, :HD, cols] = dv.T
                prod = dv.astype(F32) * ov.astype(F32)
                dt[half, HD:, cols] = split3(-jnp.sum(prod.T, axis=0, keepdims=True))
        return 0

    for half in range(2):
        own_copy(0, half).wait()
    lax.fori_loop(0, 2, lambda half, _: (prepare_q(half, core), 0)[1], 0)
    relay(heavy, 0, 0)
    relay(light, 0, 1)
    for half in range(2):
        sib_copy(0, half).wait_recv()
    lax.fori_loop(0, 2, lambda half, _: (prepare_q(half, other), 0)[1], 0)
    relay(heavy, 1, 0)
    relay(light, 1, 1)
    for kv in range(2):
        relay(light, kv, 2)
    for a in (1, 2):
        for half in range(2):
            own_copy(a, half).wait()
            sib_copy(a, half).wait_recv()
    lax.fori_loop(0, 2, prepare_d, 0)

    lane = lax.broadcasted_iota(jnp.int32, (CK, HD), 1)
    ones3 = jnp.where(lane < 3, 1.0, 0.0).astype(BF16)

    def allowed_at(tile):
        key = lax.broadcasted_iota(jnp.int32, (TOK, CB), 0)
        tok = lax.rem(lax.broadcasted_iota(jnp.int32, (TOK, CB), 1), TOK)
        return key - tok <= (n - tile) * TOK

    def return_copy(half, w):
        yy = yy_of(half)
        same = lax.div(w, 16) == yy
        cw, yhw, xw = lax.rem(lax.div(w, 8), 2), lax.rem(lax.div(w, 4), 2), lax.rem(w, 4)
        k = jnp.where(core == 0, 4 * cw + xw, 2 * cw + yhw + jnp.where(same, 0, 4))
        t = jnp.where(core == 0, jnp.where(same, 0, 1 + yh), lax.rem(x - xw + 3, 4))
        to_hp = jnp.where((core == 0) & jnp.logical_not(same), hp - 1, hp)
        to_n = jnp.where(core == 0, 4 * yhw + x, 4 * yh + xw)
        return remote(
            ret.at[half, w], r1buf.at[half, k, t], r1_send.at[half, w], r1_recv.at[half, k, t],
            dev(to_hp, core, to_n))

    def owner_copy(half, k):
        w, _ = relay_block(half, k)
        cw, yhw, xw = lax.rem(lax.div(w, 8), 2), lax.rem(lax.div(w, 4), 2), lax.rem(w, 4)
        r = jnp.where(core == 0, x, yh + 2 * lax.div(k, 4))
        to_hp = jnp.where((core == 1) & (k >= 4), hp - 1, hp)
        return remote(
            rsum.at[half, k], r2buf.at[half, core, r], r2_send.at[half, k], r2_recv.at[half, core, r],
            dev(to_hp, cw, 4 * yhw + xw))

    def relay_sums(half):
        own, last = own_of(half), last_of(half)

        def one(k, _):
            w, valid = relay_block(half, k)

            @pl.when(valid)
            def _():
                sum_kv[...] = jnp.zeros((2, TOK, HD), F32)

                @pl.when(w <= last)
                def _():
                    sum_kv[...] = ret[half, w].astype(F32)

            for t in range(3):
                to, needed = relay_peer(half, k, t)

                @pl.when(needed)
                def _():
                    remote(
                        ret.at[half, 0], r1buf.at[half, k, t], r1_send.at[half, 0], r1_recv.at[half, k, t],
                        to).wait_recv()
                    sum_kv[...] += r1buf[half, k, t].astype(F32)

            @pl.when(valid & (w != own))
            def _():
                rsum[half, k] = sum_kv[...].astype(BF16)
                owner_copy(half, k).start()

            @pl.when(w == own)
            def _():
                r2buf[half, core, jnp.where(core == 0, x, yh)] = sum_kv[...].astype(BF16)

            return 0

        lax.fori_loop(0, 8, one, 0)

    def one_half(step, _):
        half = jnp.where(step == 0, heavy, light)
        pos0 = 16 * yy_of(half) + n
        last = pos0 + 8
        n1 = lax.div(last, CH) + 1

        def by_mask(j, work):
            half_cols = QC // CB

            @pl.when(j == n1 - 1)
            def _():
                work(range(half_cols, 2 * half_cols), range(half_cols, 2 * half_cols))

            @pl.when(j == n1 - 2)
            def _():
                work(range(2 * half_cols), range(half_cols))

            @pl.when(j < n1 - 2)
            def _():
                work(range(2 * half_cols), ())

        def stats(i, _):
            j = n1 - 1 - i
            for u in range(CH):
                w = j * CH + u
                passed = is_relay(half, w)

                @pl.when((w <= last) & jnp.logical_not(passed))
                def _():
                    arrival(half, 0, w).wait_recv()

                @pl.when((w > last) & jnp.logical_not(passed))
                def _():
                    for kv in range(2):
                        kvwin[half, kv, w] = jnp.zeros((TOK, HD), BF16)

            def work(pieces, masked):
                keys = kvwin[half, 0, pl.ds(j * CH, CH)].reshape(CK, HD)
                for piece in pieces:
                    cols = slice(piece * CB, (piece + 1) * CB)
                    top, total = m8[:, cols], l8[:, cols]
                    for tile in range(CH):
                        rows = slice(tile * TOK, (tile + 1) * TOK)
                        s = jnp.dot(keys[rows], qt[half, :, cols], preferred_element_type=F32)
                        if piece in masked:
                            s = jnp.where(allowed_at(tile), s, NEG)
                        s = s.reshape(TOK // 8, 8, CB)
                        new = jnp.maximum(top, jnp.max(s, axis=0))
                        e = jnp.exp2((s - new[None]) * C2)
                        total = total * jnp.exp2((top - new) * C2) + jnp.sum(e, axis=0)
                        top = new
                        probs[j, rows, cols] = e.reshape(TOK, CB).astype(BF16)
                        m_at[j, tile, :, cols] = new
                    m8[:, cols] = top
                    l8[:, cols] = total

            by_mask(j, work)
            return 0

        m8[...] = jnp.full((8, 2 * QC), NEG, F32)
        l8[...] = jnp.zeros((8, 2 * QC), F32)
        dqt[half] = jnp.zeros((HD, 2 * QC), F32)
        lax.fori_loop(0, n1, stats, 0)
        top = jnp.max(m8[...], axis=0, keepdims=True)
        total = jnp.sum(l8[...] * jnp.exp2((m8[...] - top) * C2), axis=0, keepdims=True)
        m8[...] = jnp.broadcast_to(top, (8, 2 * QC))
        l8[...] = jnp.broadcast_to(1.0 / total, (8, 2 * QC))

        @pl.when(step == 1)
        def _():
            relay_sums(heavy)

        def grads(i, _):
            j = jnp.where(step == 0, n1 - 1 - i, i)
            for u in range(CH):
                w = j * CH + u

                @pl.when((w <= last) & jnp.logical_not(is_relay(half, w)))
                def _():
                    arrival(half, 1, w).wait_recv()

            def work(pieces, masked):
                vals = kvwin[half, 1, pl.ds(j * CH, CH)].reshape(CK, HD)
                keys_t = kvwin[half, 0, pl.ds(j * CH, CH)].reshape(CK, HD).T
                vals_1 = jnp.concatenate([vals, ones3], axis=1)
                for piece in pieces:
                    cols = slice(piece * CB, (piece + 1) * CB)
                    scale = jnp.exp2((m_at[j, :, :, cols] - m8[:, cols][None]) * C2) * l8[:, cols][None]
                    e = probs[j, :, cols].astype(F32).reshape(CH, TOK // 8, 8, CB)
                    prob = (e * scale[:, None]).reshape(CK, CB)
                    dp = jnp.dot(vals_1, dt[half, :, cols], preferred_element_type=F32)
                    probs[j, :, cols] = prob.astype(BF16)
                    dscores[:, cols] = (prob * dp).astype(BF16)
                both = slice(pieces[0] * CB, (pieces[-1] + 1) * CB)
                acc_v[...] = jnp.dot(probs[j, :, both], do_rows[half, both, :], preferred_element_type=F32)
                acc_k[...] = jnp.dot(dscores[:, both], q_rows[half, both, :], preferred_element_type=F32)
                dqt[half, :, both] += jnp.dot(keys_t, dscores[:, both], preferred_element_type=F32)

            by_mask(j, work)
            for u in range(CH):
                w = j * CH + u

                @pl.when(w <= last)
                def _():
                    rows = slice(u * TOK, (u + 1) * TOK)
                    ret[half, w, 0] = (acc_k[rows] * SCALE).astype(BF16)
                    ret[half, w, 1] = acc_v[rows].astype(BF16)

                    @pl.when(jnp.logical_not(is_relay(half, w)))
                    def _():
                        return_copy(half, w).start()

            return 0

        lax.fori_loop(0, n1, grads, 0)

        for b in range(2):
            for h in range(REP):
                cols = slice(h * HD, (h + 1) * HD)
                mine = slice(b * QC + h * HD, b * QC + (h + 1) * HD)
                dq_st[half, b, :, cols] = (dqt[half, :, mine] * SCALE).T.astype(BF16)
        dq_own(half).start()
        dq_sib(half).start()
        return 0

    def dq_own(half):
        return pltpu.make_async_copy(dq_st.at[half, core], dq_out.at[:, half_cols(half, core)], d_loc.at[half])

    def dq_sib(half):
        return remote(
            dq_st.at[half, other], dq_out.at[:, half_cols(half, core)], d_send.at[half], d_recv.at[half],
            dev(hp, other, n))

    lax.fori_loop(0, 2, one_half, 0)
    relay_sums(light)

    for half in range(2):
        for cc in range(2):
            sum_kv[...] = jnp.zeros((2, TOK, HD), F32)
            for r in range(4):
                mine = (core == cc) & (r == jnp.where(core == 0, x, yh))
                there = (cc == 0) | (r < 2) | (yy_of(half) == 0)

                @pl.when(there & jnp.logical_not(mine))
                def _():
                    remote(
                        rsum.at[half, 0], r2buf.at[half, cc, r], r2_send.at[half, 0], r2_recv.at[half, cc, r],
                        dev(hp, other, n)).wait_recv()

                @pl.when(there)
                def _():
                    sum_kv[...] += r2buf[half, cc, r].astype(F32)

            g = 2 * half + cc
            dk_out[:, g * HD : (g + 1) * HD] = sum_kv[0].astype(BF16)
            dv_out[:, g * HD : (g + 1) * HD] = sum_kv[1].astype(BF16)

    for half in range(2):
        for a in range(3):
            sib_copy(a, half).wait_send()
        for kv in range(2):
            each_source(half, kv, False, lambda copy: copy.wait_send())

            each_source(light, kv, True, lambda copy: copy.wait_send()) if half else None

        def drain_relay(k, _):
            w, valid = relay_block(half, k)
            for kv in range(2):
                pass_on(half, kv, k, w, (0, 1, 2), lambda copy: copy.wait_send())

            @pl.when(valid & (w != own_of(half)))
            def _():
                owner_copy(half, k).wait_send()

            return 0

        lax.fori_loop(0, 8, drain_relay, 0)

        def drain(w, _):
            @pl.when(jnp.logical_not(is_relay(half, w)))
            def _():
                return_copy(half, w).wait_send()

            return 0

        lax.fori_loop(0, last_of(half) + 1, drain, 0)
        dq_own(half).wait()
        dq_sib(half).wait()


def body(queries, keys, values, dout, attn_out):
    nhp = lax.axis_size("outer") // 2
    anywhere = pl.BlockSpec(memory_space=pl.ANY)
    vmem = pl.BlockSpec(memory_space=pltpu.VMEM)
    dma = pltpu.SemaphoreType.DMA
    return pl.pallas_call(
        functools.partial(kernel, nhp),
        out_shape=(
            jax.ShapeDtypeStruct(queries.shape, BF16),
            jax.ShapeDtypeStruct(keys.shape, BF16),
            jax.ShapeDtypeStruct(values.shape, BF16),
        ),
        in_specs=[anywhere, vmem, vmem, anywhere, anywhere],
        out_specs=(anywhere, vmem, vmem),
        scratch_shapes=[
            pltpu.VMEM((2, 2, 2, TOK, HD), BF16),
            pltpu.VMEM((2, 2, 32, TOK, HD), BF16),
            pltpu.VMEM((2, 32, 2, TOK, HD), BF16),
            pltpu.VMEM((2, 8, 3, 2, TOK, HD), BF16),
            pltpu.VMEM((2, 8, 2, TOK, HD), BF16),
            pltpu.VMEM((2, 2, 4, 2, TOK, HD), BF16),
            pltpu.VMEM((2, 2, TOK, QC), BF16),
            pltpu.VMEM((2, 2, TOK, QC), BF16),
            pltpu.VMEM((2, 2, TOK, QC), BF16),
            pltpu.VMEM((2, 2 * QC, HD), BF16),
            pltpu.VMEM((2, 2 * QC, HD), BF16),
            pltpu.VMEM((2, HD, 2 * QC), BF16),
            pltpu.VMEM((2, 2 * HD, 2 * QC), BF16),
            pltpu.VMEM((2, HD, 2 * QC), F32),
            pltpu.VMEM((2, 2, TOK, QC), BF16),
            pltpu.VMEM((8, 2 * QC), F32),
            pltpu.VMEM((8, 2 * QC), F32),
            pltpu.VMEM((32 // CH, CH, 8, 2 * QC), F32),
            pltpu.VMEM((32 // CH, CK, 2 * QC), BF16),
            pltpu.VMEM((CK, 2 * QC), BF16),
            pltpu.VMEM((CK, HD), F32),
            pltpu.VMEM((CK, HD), F32),
            pltpu.VMEM((2, TOK, HD), F32),
            dma((3, 2)),
            dma((3, 2)),
            dma((3, 2)),
            dma((2, 2, 2, 4)),
            dma((2, 2, 8, 3)),
            dma((2, 2, 32)),
            dma((2, 32)),
            dma((2, 8, 3)),
            dma((2, 8)),
            dma((2, 2, 4)),
            dma((2,)),
            dma((2,)),
            dma((2,)),
        ],
        compiler_params=pltpu.CompilerParams(
            collective_id=0, has_side_effects=True, vmem_limit_bytes=56 * 2**20),
        cost_estimate=pl.CostEstimate(
            flops=12_000_000_000, bytes_accessed=6_000_000, transcendentals=16_000_000),
    )(queries, keys, values, dout, attn_out)


def solution(mesh):
    rows = P(("outer", "inner"), None)
    return jax.shard_map(
        body, mesh=mesh, in_specs=(rows,) * 5, out_specs=(rows,) * 3, check_vma=False)
```

```python
import functools

import jax
import jax.numpy as jnp
from jax import lax
from jax.experimental import pallas as pl
from jax.experimental.pallas import tpu as pltpu
from jax.sharding import PartitionSpec as P

HD = 128
REP = 8
TOK = 128
QC = REP * TOK
CH = 8
CK = CH * TOK
CB = 256
SCALE = HD**-0.5
C2 = SCALE * 1.4426950408889634
NEG = -1e30
MESH = pl.DeviceIdType.MESH
F32 = jnp.float32
BF16 = jnp.bfloat16


def split3(x):
    hi = x.astype(BF16).astype(F32)
    rest = x - hi
    mid = rest.astype(BF16).astype(F32)
    low = rest - mid
    row = lax.broadcasted_iota(jnp.int32, (HD, x.shape[1]), 0)
    out = jnp.where(row == 0, hi, jnp.where(row == 1, mid, jnp.where(row == 2, low, 0.0)))
    return out.astype(BF16)


def kernel(
    nhp,
    q_in, k_in, v_in, do_in, o_in,
    dq_out, dk_out, dv_out,
    kvpack, kvwin, ret, r1buf, rsum, r2buf, q_st, do_st, o_st, q_rows, do_rows, qt, dt, dqt, dq_st,
    m8, l8, m_at, probs, dscores, acc_k, acc_v, sum_kv,
    x_loc, x_send, x_recv, s_send, f_send, g_recv, r1_send, r1_recv, r2_send, r2_recv, d_loc, d_send, d_recv,
):
    outer = lax.axis_index("outer")
    n = lax.axis_index("inner")
    core = lax.rem(outer, 2)
    other = 1 - core
    hp = lax.div(outer, 2)
    y_lo = lax.rem(hp, 2)
    x, yh = lax.rem(n, 4), lax.div(n, 4)
    across = lax.rem(n + 4, 8)
    heavy, light = 1 - y_lo, y_lo

    def dev(hp_, core_, n_):
        return (lax.rem(hp_ + nhp, nhp) * 2 + core_, n_)

    def half_cols(half, cc):
        return pl.ds(pl.multiple_of(half * (2 * QC) + cc * QC, QC), QC)

    def yy_of(half):
        return jnp.where(half == 0, y_lo, 1 - y_lo)

    def own_of(half):
        return 16 * yy_of(half) + 8 * core + n

    def last_of(half):
        return 16 * yy_of(half) + 8 + n

    def remote(src, dst, send, recv, to):
        return pltpu.make_async_remote_copy(
            src_ref=src, dst_ref=dst, send_sem=send, recv_sem=recv, device_id=to, device_id_type=MESH)

    sources = ((q_in, q_st), (do_in, do_st), (o_in, o_st))

    def own_copy(a, half):
        src, dst = sources[a]
        return pltpu.make_async_copy(src.at[:, half_cols(half, core)], dst.at[half, core], x_loc.at[a, half])

    def sib_copy(a, half):
        src, dst = sources[a]
        return remote(
            src.at[:, half_cols(half, other)], dst.at[half, core],
            x_send.at[a, half], x_recv.at[a, half], dev(hp, other, n))

    barrier = pltpu.get_barrier_semaphore()
    chips = [(hp, 4 * yh + lax.rem(x + t, 4)) for t in (1, 2, 3)] + [(hp, across)]
    chips += [(hp + 1, x), (hp + 1, 4 + x), (hp - 1, x), (hp - 1, 4 + x)]
    greeted = [dev(hp, other, n)] + [dev(h_, cc, n_) for h_, n_ in chips for cc in range(2)]
    for to in greeted:
        pl.semaphore_signal(barrier, inc=1, device_id=to, device_id_type=MESH)

    for a in range(3):
        for half in range(2):
            own_copy(a, half).start()
    for half in range(2):
        for cc in range(2):
            g = 2 * half + cc
            kvpack[half, cc, 0] = k_in[:, g * HD : (g + 1) * HD]
            kvpack[half, cc, 1] = v_in[:, g * HD : (g + 1) * HD]
    for half in range(2):
        for kv in range(2):
            kvwin[half, kv, own_of(half)] = kvpack[half, core, kv]

    pl.semaphore_wait(barrier, len(greeted))

    def each_source(half, kv, late, act):
        yy, own = yy_of(half), own_of(half)

        def send(cc, slot, to_hp, nn):
            act(remote(
                kvpack.at[half, cc, kv], kvwin.at[half, kv, own],
                s_send.at[half, kv, cc, slot], g_recv.at[half, kv, own], dev(to_hp, cc, nn)))

        if not late:
            for cc in range(2):
                @pl.when(core != cc)
                def _():
                    send(cc, 3, hp, n)

            for t in range(3):
                send(0, t, hp, 4 * yh + lax.rem(x + 1 + t, 4))

            @pl.when(yy == 0)
            def _():
                send(1, 1, hp + 1, x)
                send(1, 2, hp + 1, 4 + x)

        @pl.when(yy == (0 if late else 1))
        def _():
            send(1, 0, hp, across)

    def relay_block(half, k):
        yy = yy_of(half)
        w0 = 16 * yy + 8 * lax.div(k, 4) + 4 * yh + lax.rem(k, 4)
        w1 = 16 * (yy - lax.div(k, 4)) + 8 * lax.rem(lax.div(k, 2), 2) + 4 * lax.rem(k, 2) + x
        return jnp.where(core == 0, w0, w1), (core == 0) | (k < 4) | (yy == 1)

    def relay_peer(half, k, t):
        yy = yy_of(half)
        w, valid = relay_block(half, k)
        n1 = 4 * yh + lax.rem(x + 1 + t, 4)
        if t == 0:
            needed0 = w <= 16 * yy + 8 + across
            hp0, n0 = hp, across
        else:
            needed0 = yy == 0
            hp0, n0 = hp + 1, 4 * (t - 1) + x
        needed1 = w <= 16 * yy + 8 + n1
        to = dev(jnp.where(core == 0, hp0, hp), core, jnp.where(core == 0, n0, n1))
        return to, valid & (((core == 0) & needed0) | ((core == 1) & needed1))

    def is_relay(half, w):
        yy = yy_of(half)
        row = (lax.div(w, 16) == yy) & (lax.rem(lax.div(w, 4), 2) == yh)
        return ((core == 0) & row) | ((core == 1) & (lax.rem(w, 4) == x))

    def arrival(half, kv, w):
        return remote(
            kvpack.at[half, 0, kv], kvwin.at[half, kv, w], s_send.at[half, kv, 0, 0],
            g_recv.at[half, kv, w], dev(hp, other, n))

    def pass_on(half, kv, k, w, peers, act):
        for t in peers:
            to, needed = relay_peer(half, k, t)

            @pl.when(needed)
            def _():
                block = kvwin.at[half, kv, w]
                act(remote(block, block, f_send.at[half, kv, k, t], g_recv.at[half, kv, w], to))

    def relay(half, kv, part):
        def one(k, _):
            w, valid = relay_block(half, k)

            @pl.when(valid & (w != own_of(half)))
            def _():
                arrival(half, kv, w).wait_recv()

            pass_on(half, kv, k, w, (0, 1, 2) if part == 0 else (1, 2), lambda copy: copy.start())
            return 0

        def again(k, _):
            w, _ = relay_block(half, k)
            pass_on(half, kv, k, w, (0,), lambda copy: copy.start())
            return 0

        if part == 0:
            lax.fori_loop(0, 8, one, 0)
        elif part == 1:
            @pl.when(core == 0)
            def _():
                lax.fori_loop(0, 8, one, 0)
        else:
            @pl.when(core == 0)
            def _():
                lax.fori_loop(0, 8, again, 0)

            @pl.when(core == 1)
            def _():
                def column(k, _):
                    w, valid = relay_block(half, k)

                    @pl.when(valid & (w != own_of(half)))
                    def _():
                        arrival(half, kv, w).wait_recv()

                    pass_on(half, kv, k, w, (0, 1, 2), lambda copy: copy.start())
                    return 0

                lax.fori_loop(0, 8, column, 0)

    start = lambda copy: copy.start()
    for half in (heavy, light):
        sib_copy(0, half).start()
    for kv in range(2):
        for half in (heavy, light):
            each_source(half, kv, False, start)
    for kv in range(2):
        each_source(light, kv, True, start)
    for a in (1, 2):
        for half in (heavy, light):
            sib_copy(a, half).start()

    def prepare_q(half, b):
        for h in range(REP):
            qv = q_st[half, b, :, h * HD : (h + 1) * HD]
            cols = pl.ds(pl.multiple_of(b * QC + h * HD, HD), HD)
            q_rows[half, cols, :] = qv
            qt[half, :, cols] = qv.T

    def prepare_d(half, _):
        for b in range(2):
            for h in range(REP):
                dv = do_st[half, b, :, h * HD : (h + 1) * HD]
                ov = o_st[half, b, :, h * HD : (h + 1) * HD]
                cols = slice(b * QC + h * HD, b * QC + (h + 1) * HD)
                do_rows[half, cols, :] = dv
                dt[half, :HD, cols] = dv.T
                prod = dv.astype(F32) * ov.astype(F32)
                dt[half, HD:, cols] = split3(-jnp.sum(prod.T, axis=0, keepdims=True))
        return 0

    for half in range(2):
        own_copy(0, half).wait()
    lax.fori_loop(0, 2, lambda half, _: (prepare_q(half, core), 0)[1], 0)
    relay(heavy, 0, 0)
    relay(light, 0, 1)
    for half in range(2):
        sib_copy(0, half).wait_recv()
    lax.fori_loop(0, 2, lambda half, _: (prepare_q(half, other), 0)[1], 0)
    relay(heavy, 1, 0)
    relay(light, 1, 1)
    for kv in range(2):
        relay(light, kv, 2)
    for a in (1, 2):
        for half in range(2):
            own_copy(a, half).wait()
            sib_copy(a, half).wait_recv()
    lax.fori_loop(0, 2, prepare_d, 0)

    lane = lax.broadcasted_iota(jnp.int32, (CK, HD), 1)
    ones3 = jnp.where(lane < 3, 1.0, 0.0).astype(BF16)

    def allowed_at(tile):
        key = lax.broadcasted_iota(jnp.int32, (TOK, CB), 0)
        tok = lax.rem(lax.broadcasted_iota(jnp.int32, (TOK, CB), 1), TOK)
        return key - tok <= (n - tile) * TOK

    def return_copy(half, w):
        yy = yy_of(half)
        same = lax.div(w, 16) == yy
        cw, yhw, xw = lax.rem(lax.div(w, 8), 2), lax.rem(lax.div(w, 4), 2), lax.rem(w, 4)
        k = jnp.where(core == 0, 4 * cw + xw, 2 * cw + yhw + jnp.where(same, 0, 4))
        t = jnp.where(core == 0, jnp.where(same, 0, 1 + yh), lax.rem(x - xw + 3, 4))
        to_hp = jnp.where((core == 0) & jnp.logical_not(same), hp - 1, hp)
        to_n = jnp.where(core == 0, 4 * yhw + x, 4 * yh + xw)
        return remote(
            ret.at[half, w], r1buf.at[half, k, t], r1_send.at[half, w], r1_recv.at[half, k, t],
            dev(to_hp, core, to_n))

    def owner_copy(half, k):
        w, _ = relay_block(half, k)
        cw, yhw, xw = lax.rem(lax.div(w, 8), 2), lax.rem(lax.div(w, 4), 2), lax.rem(w, 4)
        r = jnp.where(core == 0, x, yh + 2 * lax.div(k, 4))
        to_hp = jnp.where((core == 1) & (k >= 4), hp - 1, hp)
        return remote(
            rsum.at[half, k], r2buf.at[half, core, r], r2_send.at[half, k], r2_recv.at[half, core, r],
            dev(to_hp, cw, 4 * yhw + xw))

    def relay_sums(half):
        own, last = own_of(half), last_of(half)

        def one(k, _):
            w, valid = relay_block(half, k)

            @pl.when(valid)
            def _():
                sum_kv[...] = jnp.zeros((2, TOK, HD), F32)

                @pl.when(w <= last)
                def _():
                    sum_kv[...] = ret[half, w].astype(F32)

            for t in range(3):
                to, needed = relay_peer(half, k, t)

                @pl.when(needed)
                def _():
                    remote(
                        ret.at[half, 0], r1buf.at[half, k, t], r1_send.at[half, 0], r1_recv.at[half, k, t],
                        to).wait_recv()
                    sum_kv[...] += r1buf[half, k, t].astype(F32)

            @pl.when(valid & (w != own))
            def _():
                rsum[half, k] = sum_kv[...].astype(BF16)
                owner_copy(half, k).start()

            @pl.when(w == own)
            def _():
                r2buf[half, core, jnp.where(core == 0, x, yh)] = sum_kv[...].astype(BF16)

            return 0

        lax.fori_loop(0, 8, one, 0)

    def one_half(step, _):
        half = jnp.where(step == 0, heavy, light)
        pos0 = 16 * yy_of(half) + n
        last = pos0 + 8
        n1 = lax.div(last, CH) + 1

        def by_mask(j, work):
            half_cols = QC // CB

            @pl.when(j == n1 - 1)
            def _():
                work(range(half_cols, 2 * half_cols), range(half_cols, 2 * half_cols))

            @pl.when(j == n1 - 2)
            def _():
                work(range(2 * half_cols), range(half_cols))

            @pl.when(j < n1 - 2)
            def _():
                work(range(2 * half_cols), ())

        def stats(i, _):
            j = n1 - 1 - i
            for u in range(CH):
                w = j * CH + u
                passed = is_relay(half, w)

                @pl.when((w <= last) & jnp.logical_not(passed))
                def _():
                    arrival(half, 0, w).wait_recv()

                @pl.when((w > last) & jnp.logical_not(passed))
                def _():
                    for kv in range(2):
                        kvwin[half, kv, w] = jnp.zeros((TOK, HD), BF16)

            def work(pieces, masked):
                keys = kvwin[half, 0, pl.ds(j * CH, CH)].reshape(CK, HD)
                for piece in pieces:
                    cols = slice(piece * CB, (piece + 1) * CB)
                    top, total = m8[:, cols], l8[:, cols]
                    for tile in range(CH):
                        rows = slice(tile * TOK, (tile + 1) * TOK)
                        s = jnp.dot(keys[rows], qt[half, :, cols], preferred_element_type=F32)
                        if piece in masked:
                            s = jnp.where(allowed_at(tile), s, NEG)
                        s = s.reshape(TOK // 8, 8, CB)
                        new = jnp.maximum(top, jnp.max(s, axis=0))
                        e = jnp.exp2((s - new[None]) * C2)
                        total = total * jnp.exp2((top - new) * C2) + jnp.sum(e, axis=0)
                        top = new
                        probs[j, rows, cols] = e.reshape(TOK, CB).astype(BF16)
                        m_at[j, tile, :, cols] = new
                    m8[:, cols] = top
                    l8[:, cols] = total

            by_mask(j, work)
            return 0

        m8[...] = jnp.full((8, 2 * QC), NEG, F32)
        l8[...] = jnp.zeros((8, 2 * QC), F32)
        dqt[half] = jnp.zeros((HD, 2 * QC), F32)
        lax.fori_loop(0, n1, stats, 0)
        top = jnp.max(m8[...], axis=0, keepdims=True)
        total = jnp.sum(l8[...] * jnp.exp2((m8[...] - top) * C2), axis=0, keepdims=True)
        m8[...] = jnp.broadcast_to(top, (8, 2 * QC))
        l8[...] = jnp.broadcast_to(1.0 / total, (8, 2 * QC))

        @pl.when(step == 1)
        def _():
            relay_sums(heavy)

        def grads(i, _):
            j = i
            for u in range(CH):
                w = j * CH + u

                @pl.when((w <= last) & jnp.logical_not(is_relay(half, w)))
                def _():
                    arrival(half, 1, w).wait_recv()

            def work(pieces, masked):
                vals = kvwin[half, 1, pl.ds(j * CH, CH)].reshape(CK, HD)
                keys_t = kvwin[half, 0, pl.ds(j * CH, CH)].reshape(CK, HD).T
                vals_1 = jnp.concatenate([vals, ones3], axis=1)
                for piece in pieces:
                    cols = slice(piece * CB, (piece + 1) * CB)
                    scale = jnp.exp2((m_at[j, :, :, cols] - m8[:, cols][None]) * C2) * l8[:, cols][None]
                    e = probs[j, :, cols].astype(F32).reshape(CH, TOK // 8, 8, CB)
                    prob = (e * scale[:, None]).reshape(CK, CB)
                    dp = jnp.dot(vals_1, dt[half, :, cols], preferred_element_type=F32)
                    probs[j, :, cols] = prob.astype(BF16)
                    dscores[:, cols] = (prob * dp).astype(BF16)
                both = slice(pieces[0] * CB, (pieces[-1] + 1) * CB)
                acc_v[...] = jnp.dot(probs[j, :, both], do_rows[half, both, :], preferred_element_type=F32)
                acc_k[...] = jnp.dot(dscores[:, both], q_rows[half, both, :], preferred_element_type=F32)
                dqt[half, :, both] += jnp.dot(keys_t, dscores[:, both], preferred_element_type=F32)

            by_mask(j, work)
            for u in range(CH):
                w = j * CH + u

                @pl.when(w <= last)
                def _():
                    rows = slice(u * TOK, (u + 1) * TOK)
                    ret[half, w, 0] = (acc_k[rows] * SCALE).astype(BF16)
                    ret[half, w, 1] = acc_v[rows].astype(BF16)

                    @pl.when(jnp.logical_not(is_relay(half, w)))
                    def _():
                        return_copy(half, w).start()

            return 0

        lax.fori_loop(0, n1, grads, 0)

        for b in range(2):
            for h in range(REP):
                cols = slice(h * HD, (h + 1) * HD)
                mine = slice(b * QC + h * HD, b * QC + (h + 1) * HD)
                dq_st[half, b, :, cols] = (dqt[half, :, mine] * SCALE).T.astype(BF16)
        dq_own(half).start()
        dq_sib(half).start()
        return 0

    def dq_own(half):
        return pltpu.make_async_copy(dq_st.at[half, core], dq_out.at[:, half_cols(half, core)], d_loc.at[half])

    def dq_sib(half):
        return remote(
            dq_st.at[half, other], dq_out.at[:, half_cols(half, core)], d_send.at[half], d_recv.at[half],
            dev(hp, other, n))

    lax.fori_loop(0, 2, one_half, 0)
    relay_sums(light)

    for half in range(2):
        for cc in range(2):
            sum_kv[...] = jnp.zeros((2, TOK, HD), F32)
            for r in range(4):
                mine = (core == cc) & (r == jnp.where(core == 0, x, yh))
                there = (cc == 0) | (r < 2) | (yy_of(half) == 0)

                @pl.when(there & jnp.logical_not(mine))
                def _():
                    remote(
                        rsum.at[half, 0], r2buf.at[half, cc, r], r2_send.at[half, 0], r2_recv.at[half, cc, r],
                        dev(hp, other, n)).wait_recv()

                @pl.when(there)
                def _():
                    sum_kv[...] += r2buf[half, cc, r].astype(F32)

            g = 2 * half + cc
            dk_out[:, g * HD : (g + 1) * HD] = sum_kv[0].astype(BF16)
            dv_out[:, g * HD : (g + 1) * HD] = sum_kv[1].astype(BF16)

    for half in range(2):
        for a in range(3):
            sib_copy(a, half).wait_send()
        for kv in range(2):
            each_source(half, kv, False, lambda copy: copy.wait_send())

            each_source(light, kv, True, lambda copy: copy.wait_send()) if half else None

        def drain_relay(k, _):
            w, valid = relay_block(half, k)
            for kv in range(2):
                pass_on(half, kv, k, w, (0, 1, 2), lambda copy: copy.wait_send())

            @pl.when(valid & (w != own_of(half)))
            def _():
                owner_copy(half, k).wait_send()

            return 0

        lax.fori_loop(0, 8, drain_relay, 0)

        def drain(w, _):
            @pl.when(jnp.logical_not(is_relay(half, w)))
            def _():
                return_copy(half, w).wait_send()

            return 0

        lax.fori_loop(0, last_of(half) + 1, drain, 0)
        dq_own(half).wait()
        dq_sib(half).wait()


def body(queries, keys, values, dout, attn_out):
    nhp = lax.axis_size("outer") // 2
    anywhere = pl.BlockSpec(memory_space=pl.ANY)
    vmem = pl.BlockSpec(memory_space=pltpu.VMEM)
    dma = pltpu.SemaphoreType.DMA
    return pl.pallas_call(
        functools.partial(kernel, nhp),
        out_shape=(
            jax.ShapeDtypeStruct(queries.shape, BF16),
            jax.ShapeDtypeStruct(keys.shape, BF16),
            jax.ShapeDtypeStruct(values.shape, BF16),
        ),
        in_specs=[anywhere, vmem, vmem, anywhere, anywhere],
        out_specs=(anywhere, vmem, vmem),
        scratch_shapes=[
            pltpu.VMEM((2, 2, 2, TOK, HD), BF16),
            pltpu.VMEM((2, 2, 32, TOK, HD), BF16),
            pltpu.VMEM((2, 32, 2, TOK, HD), BF16),
            pltpu.VMEM((2, 8, 3, 2, TOK, HD), BF16),
            pltpu.VMEM((2, 8, 2, TOK, HD), BF16),
            pltpu.VMEM((2, 2, 4, 2, TOK, HD), BF16),
            pltpu.VMEM((2, 2, TOK, QC), BF16),
            pltpu.VMEM((2, 2, TOK, QC), BF16),
            pltpu.VMEM((2, 2, TOK, QC), BF16),
            pltpu.VMEM((2, 2 * QC, HD), BF16),
            pltpu.VMEM((2, 2 * QC, HD), BF16),
            pltpu.VMEM((2, HD, 2 * QC), BF16),
            pltpu.VMEM((2, 2 * HD, 2 * QC), BF16),
            pltpu.VMEM((2, HD, 2 * QC), F32),
            pltpu.VMEM((2, 2, TOK, QC), BF16),
            pltpu.VMEM((8, 2 * QC), F32),
            pltpu.VMEM((8, 2 * QC), F32),
            pltpu.VMEM((32 // CH, CH, 8, 2 * QC), F32),
            pltpu.VMEM((32 // CH, CK, 2 * QC), BF16),
            pltpu.VMEM((CK, 2 * QC), BF16),
            pltpu.VMEM((CK, HD), F32),
            pltpu.VMEM((CK, HD), F32),
            pltpu.VMEM((2, TOK, HD), F32),
            dma((3, 2)),
            dma((3, 2)),
            dma((3, 2)),
            dma((2, 2, 2, 4)),
            dma((2, 2, 8, 3)),
            dma((2, 2, 32)),
            dma((2, 32)),
            dma((2, 8, 3)),
            dma((2, 8)),
            dma((2, 2, 4)),
            dma((2,)),
            dma((2,)),
            dma((2,)),
        ],
        compiler_params=pltpu.CompilerParams(
            collective_id=0, has_side_effects=True, vmem_limit_bytes=56 * 2**20),
        cost_estimate=pl.CostEstimate(
            flops=12_000_000_000, bytes_accessed=6_000_000, transcendentals=16_000_000),
    )(queries, keys, values, dout, attn_out)


def solution(mesh):
    rows = P(("outer", "inner"), None)
    return jax.shard_map(
        body, mesh=mesh, in_specs=(rows,) * 5, out_specs=(rows,) * 3, check_vma=False)
```
